32 devices in a mesh: dp: 16 (over z, y, core), tensor: 2 (over x).
Axes of the slice: x: 2, y: 2, z: 4, core: 2. Of those that a mesh axis runs over, the one named last changes fastest.
Arguments:
- residual: bfloat16 [16384, 1024], P(('dp', 'tensor')), may hold values from -6 to 6
- ln_gain: float32 [1024], replicated, may hold values from 0.1 to 1.9
- ln_bias: float32 [1024], replicated, may hold values from -1.75 to 1.75
- w_qkv: bfloat16 [1024, 3072], P(None, 'tensor'), may hold values from -0.1875 to 0.1875
- b_qkv: float32 [3072], P('tensor'), may hold values from -3 to 3
- w_out: bfloat16 [1024, 1024], P('tensor'), may hold values from -0.75 to 0.75
- b_out: float32 [1024], replicated, may hold values from -3 to 3
- w_up: bfloat16 [1024, 4096], P(None, 'tensor'), may hold values from -0.1875 to 0.1875
- b_up: float32 [4096], P('tensor'), may hold values from -3 to 3
- w_down: bfloat16 [4096, 1024], P('tensor'), may hold values from -0.09375 to 0.09375
- b_down: float32 [1024], replicated, may hold values from -3 to 3
- grad_out: bfloat16 [16384, 1024], P(('dp', 'tensor')), may hold values from -6 to 6
Outputs:
- out: bfloat16 [16384, 1024], P(('dp', 'tensor'))
- grad_in: float32 [16384, 1024], P(('dp', 'tensor'))
- grad_ln_gain: float32 [1024], replicated
- grad_ln_bias: float32 [1024], replicated
- grad_w_qkv: float32 [1024, 3072], P(None, 'tensor')
- grad_b_qkv: float32 [3072], P('tensor')
- grad_w_out: float32 [1024, 1024], P('tensor')
- grad_b_out: float32 [1024], replicated
- grad_w_up: float32 [1024, 4096], P(None, 'tensor')
- grad_b_up: float32 [4096], P('tensor')
- grad_w_down: float32 [4096, 1024], P('tensor')
- grad_b_down: float32 [1024], replicated
The draws below stay inside these ranges and needn't reach their ends.
All inputs are finite; a program needn't handle non-finite values.
Results may differ from the reference program's by a relative error of at most 0.012.
Values may be sent and summed in bfloat16 or wider, within the bound.
A program may use at most 256 MiB of HBM per device.

```python
import math
import jax
import jax.numpy as jnp
from jax import lax

D = 1024
H = 16
HD = 64
ROT = 16
FF = 4096
SEQLEN = 1024
TOKENS = 16384


def shard_levels(key, dims, cuts, smallest, top_value):
    gain, own = 1.0, jax.random.fold_in(key, 6)
    for dim, blocks in cuts:
        heights = jnp.exp(jax.random.uniform(jax.random.fold_in(own, dim), (blocks,), jnp.float32, smallest / len(cuts), top_value / len(cuts)))
        gain = gain * jnp.repeat(heights, dims[dim] // blocks).reshape([-1 if axis == dim else 1 for axis in range(len(dims))])
    return gain


def normal_values(key, dims, width, reach, pieces=(), kind=jnp.bfloat16):
    values = width * jax.random.normal(key, dims, jnp.float32)
    if pieces:
        values = values * shard_levels(key, dims, pieces, -0.22, 0.18)
    return jnp.clip(values, -reach, reach).astype(kind)


def setup_inputs(seed: int = 0) -> dict:
    splits = jax.random.split(jax.random.key(seed), 13)
    return {
        "residual": normal_values(splits[0], (TOKENS, D), 1.0, 6.0, ((0, 32),)),
        "ln_gain": jnp.clip(1.0 + 0.18 * jax.random.normal(splits[1], (D,), jnp.float32), 0.1, 1.9),
        "ln_bias": normal_values(splits[2], (D,), 0.3, 1.75, (), jnp.float32),
        "w_qkv": normal_values(splits[3], (D, 3 * D), D ** -0.5, 0.1875, ((1, 2),)),
        "b_qkv": normal_values(splits[4], (3 * D,), 0.5, 3.0, ((0, 2),), jnp.float32),
        "w_out": normal_values(splits[5], (D, D), (D // 16) ** -0.5, 0.75, ((0, 2),)),
        "b_out": normal_values(splits[6], (D,), 0.5, 3.0, (), jnp.float32),
        "w_up": normal_values(splits[7], (D, FF), D ** -0.5, 0.1875, ((1, 2),)),
        "b_up": normal_values(splits[8], (FF,), 0.5, 3.0, ((0, 2),), jnp.float32),
        "w_down": normal_values(splits[9], (FF, D), FF ** -0.5, 0.09375, ((0, 2),)),
        "b_down": normal_values(splits[10], (D,), 0.5, 3.0, (), jnp.float32),
        "grad_out": normal_values(splits[11], (TOKENS, D), 1.0, 6.0, ((0, 32),)),
    }


@jax.custom_vjp
def low(v):
    return lax.optimization_barrier(v.astype(jnp.bfloat16)).astype(jnp.float32)

@jax.custom_vjp
def low_back(v):
    return v

def low_keep(v):
    return (low(v), None)

def low_pass(kept, grad):
    return (grad,)

def back_keep(v):
    return (v, None)

def back_low(kept, grad):
    return (low(grad),)
low.defvjp(low_keep, low_pass)
low_back.defvjp(back_keep, back_low)
epsilon = 1e-05

def turn_tables(seqlen):
    half_rot = ROT // 2
    exponent = jnp.arange(half_rot, dtype=jnp.float32) * (2.0 / ROT)
    inverse = 1.0 / 10000.0 ** exponent
    places = jnp.arange(seqlen, dtype=jnp.float32)
    angles = places[:, None] * inverse[None, :]
    return (jnp.cos(angles), jnp.sin(angles))

def turn_heads(heads, cosine, sine):
    half_rot = ROT // 2
    first = heads[:, :, :half_rot]
    second = heads[:, :, half_rot:ROT]
    rest = heads[:, :, ROT:]
    cos_rows = cosine[:, None, :]
    sin_rows = sine[:, None, :]
    return jnp.concatenate([first * cos_rows - second * sin_rows, second * cos_rows + first * sin_rows, rest], axis=2)

def layer(residual, ln_gain, ln_bias, w_qkv, b_qkv, w_out, b_out, w_up, b_up, w_down, b_down):
    highest = lax.Precision.HIGHEST
    average = lax.optimization_barrier(jnp.mean(residual, axis=1, keepdims=True))
    centered = residual - average
    variance = lax.optimization_barrier(jnp.mean(centered * centered, axis=1, keepdims=True))
    normed = centered * lax.rsqrt(variance + epsilon)
    hidden = low(normed * ln_gain + ln_bias)
    qkv = low_back(jnp.dot(hidden, w_qkv, precision=highest) + b_qkv)
    up_lin = low_back(jnp.dot(hidden, w_up, precision=highest) + b_up)
    act = low(jax.nn.gelu(up_lin, approximate=False))
    cosine, sine = turn_tables(SEQLEN)
    causal = jnp.arange(SEQLEN)[:, None] >= jnp.arange(SEQLEN)[None, :]
    scale = 1.0 / math.sqrt(HD)

    def attend(block):
        queries = low(turn_heads(block[:, :, 0, :], cosine, sine))
        key_rows = low(turn_heads(block[:, :, 1, :], cosine, sine))
        value_rows = low(block[:, :, 2, :])
        scores = low_back(jnp.einsum('qhd,khd->hqk', queries, key_rows, precision=highest) * scale)
        scores = jnp.where(causal[None], scores, -1e+30)
        peak = lax.optimization_barrier(jnp.max(scores, axis=2, keepdims=True))
        raised = jnp.exp(scores - peak)
        probs = raised / lax.optimization_barrier(jnp.sum(raised, axis=2, keepdims=True))
        attended = jnp.einsum('hqk,khd->qhd', low(probs), value_rows, precision=highest)
        return low_back(low(attended)).reshape(SEQLEN, H * HD)
    blocks = qkv.reshape(TOKENS // SEQLEN, SEQLEN, H, 3, HD)
    attended = lax.map(jax.checkpoint(attend), blocks).reshape(TOKENS, H * HD)
    branch_one = jnp.dot(attended, w_out, precision=highest)
    branch_two = jnp.dot(act, w_down, precision=highest)
    return residual + branch_one + b_out + branch_two + b_down

def reference(residual, ln_gain, ln_bias, w_qkv, b_qkv, w_out, b_out, w_up, b_up, w_down, b_down, grad_out):
    wide = jnp.float32
    result, pullback = jax.vjp(layer, residual.astype(wide), ln_gain.astype(wide), ln_bias.astype(wide), w_qkv.astype(wide), b_qkv.astype(wide), w_out.astype(wide), b_out.astype(wide), w_up.astype(wide), b_up.astype(wide), w_down.astype(wide), b_down.astype(wide))
    grads = pullback(grad_out.astype(wide))
    return (result.astype(jnp.bfloat16), grads[0], grads[1], grads[2], grads[3], grads[4], grads[5], grads[6], grads[7], grads[8], grads[9], grads[10])
```

```python
import functools
import math

import jax
import jax.numpy as jnp
from jax import lax
from jax.experimental import pallas as pl
from jax.experimental.pallas import tpu as pltpu
from jax.sharding import PartitionSpec as P

HD = 64
ROT = 16
LEN_MAX = 1024
epsilon = 1e-05
MESH = pl.DeviceIdType.MESH
f32 = jnp.float32
bf16 = jnp.bfloat16


def dot(left, right):
    return lax.dot_general(left, right, (((1,), (0,)), ((), ())), preferred_element_type=f32)


def dot_nt(left, right):
    return lax.dot_general(left, right, (((1,), (1,)), ((), ())), preferred_element_type=f32)


def dot_tn(left, right):
    return lax.dot_general(left, right, (((0,), (0,)), ((), ())), preferred_element_type=f32)


def turn_tables(seqlen):
    half_rot = ROT // 2
    exponent = jnp.arange(half_rot, dtype=f32) * (2.0 / ROT)
    inverse = 1.0 / 10000.0**exponent
    places = jnp.arange(seqlen, dtype=f32)
    angles = places[:, None] * inverse[None, :]
    return (jnp.cos(angles), jnp.sin(angles))


def turn(t, cos, sin, sign):
    a, b = t[0:8], t[8:16]
    return jnp.concatenate([a * cos - sign * (b * sin), b * cos + sign * (a * sin), t[16:]], axis=0)


def attend_head(q_t, k_t, v_t, do_t, cos, sin, blk=256):
    seq = q_t.shape[1]
    qs = turn(q_t, cos, sin, 1.0).astype(bf16) * jnp.asarray(0.125, bf16)
    kb = turn(k_t, cos, sin, 1.0).astype(bf16)
    vb = v_t.astype(bf16)
    keys, values, queries, grads = kb.T, vb.T, qs.T, do_t.T
    nb = seq // blk
    outs, dqs = [], []
    dv_sum, dk_sum = [None] * nb, [None] * nb
    for i in range(nb):
        kk, sl = (i + 1) * blk, slice(i * blk, (i + 1) * blk)
        s = dot(keys[:kk], qs[:, sl])
        rows = lax.broadcasted_iota(jnp.int32, (blk, blk), 0)
        cols = lax.broadcasted_iota(jnp.int32, (blk, blk), 1)
        diag = jnp.where(rows <= cols, s[i * blk :], -1e30)
        s = jnp.concatenate([s[: i * blk], diag], axis=0) if i else diag
        p = jnp.exp(s - jnp.max(s, axis=0, keepdims=True))
        p = p * (1.0 / jnp.sum(p, axis=0, keepdims=True))
        pb = p.astype(bf16)
        o = dot(vb[:, :kk], pb)
        dp = dot(values[:kk], do_t[:, sl])
        mean = jnp.sum(o * do_t[:, sl].astype(f32), axis=0, keepdims=True)
        ds = (p * (dp - mean)).astype(bf16)
        outs.append(o.astype(bf16))
        dqs.append(dot(kb[:, :kk], ds) * 0.125)
        dv, dk = dot(pb, grads[sl]), dot(ds, queries[sl])
        for j in range(i + 1):
            a, b = dv[j * blk : (j + 1) * blk], dk[j * blk : (j + 1) * blk]
            dv_sum[j] = a if dv_sum[j] is None else dv_sum[j] + a
            dk_sum[j] = b if dk_sum[j] is None else dk_sum[j] + b
    dq_t = turn(jnp.concatenate(dqs, axis=1), cos, sin, -1.0)
    dk_t = turn(jnp.concatenate(dk_sum, axis=0).T, cos, sin, -1.0)
    dv_t = jnp.concatenate(dv_sum, axis=0).T
    return jnp.concatenate(outs, axis=1), dq_t, dk_t, dv_t


RW = 256
RQ = RW // 4
NS = 6
KINDS = ("P", "A1", "A2", "A3", "A4", "A5", "B1", "B2", "B3", "B4", "B5a", "B5b", "G")
KI = {k: i for i, k in enumerate(KINDS)}


def mega_kernel(
    n_ff, heads,
    ffg, h, g, w_t, bq, wo, cs, ffb, ffd, resid, vecs, small_in,
    red, out, grad_in, small_out,
    x_buf, own, ag, fin, ra1, ra2, ra3, rb1, rb2, rb3,
    qkv_s, do_s, dqkv_t, att_t, dh_own, br_send, br_recv, dh_send, dh_recv, ff_buf, rs_buf, sm_send, sm_recv, sums,
    ss, rs, own_sem, loc_sem, x_ss, x_rs, ff_sem, sm_ss, sm_rs, fin_sem,
):
    n_at = heads // 2
    waves = n_ff + n_at
    dp, x = lax.axis_index("dp"), lax.axis_index("tensor")
    c, y, z = lax.rem(dp, 2), lax.rem(dp // 2, 2), dp // 4
    dev = lambda zz, yy, cc, xx: (zz * 4 + yy * 2 + cc, xx)
    sib = dev(z, y, 1 - c, x)
    yp = dev(z, 1 - y, c, x)
    zp = dev(z + 1 - 2 * lax.rem(z, 2), y, c, x)
    zm = dev(3 - z, y, c, x)
    xp = dev(z, y, c, 1 - x)
    inner = jnp.logical_or(z == 1, z == 2)
    outer = jnp.logical_not(inner)

    barrier = pltpu.get_barrier_semaphore()
    for d in (sib, yp, zp, zm, xp):
        pl.semaphore_signal(barrier, inc=1, device_id=d, device_id_type=MESH)
    pl.semaphore_wait(barrier, 5)

    a_mine = pl.ds(pl.multiple_of(y * RQ, RQ), RQ)
    a_other = pl.ds(pl.multiple_of((1 - y) * RQ, RQ), RQ)
    zi = jnp.where(z == 2, 1, 0)
    b_mine = pl.ds(pl.multiple_of(2 * RQ + zi * RQ, RQ), RQ)
    b_other = pl.ds(pl.multiple_of(2 * RQ + (1 - zi) * RQ, RQ), RQ)
    b_all = pl.ds(2 * RQ, 2 * RQ)

    def rc(kind, w, src, dst, device):
        k = KI[kind]
        return pltpu.make_async_remote_copy(
            src_ref=src, dst_ref=dst, send_sem=ss.at[k, w], recv_sem=rs.at[k, w], device_id=device, device_id_type=MESH
        )

    def cp(kind, w):
        s = lax.rem(w, NS)
        if kind == "A1":
            return rc(kind, w, x_buf.at[w, a_other], ra1.at[s], yp)
        if kind == "A2":
            return rc(kind, w, x_buf.at[w, a_mine], ra2.at[s], zp)
        if kind == "A3":
            return rc(kind, w, x_buf.at[w, a_mine], ra3.at[s], zm)
        if kind == "A4":
            return rc(kind, w, fin.at[w, a_mine], fin.at[w, a_mine], zp)
        if kind == "A5":
            return rc(kind, w, fin.at[w, a_mine], fin.at[w, a_mine], yp)
        if kind == "B1":
            return rc(kind, w, x_buf.at[w, b_all], rb1.at[s], zp)
        if kind == "B2":
            return rc(kind, w, x_buf.at[w, b_other], rb2.at[s], zm)
        if kind == "B3":
            return rc(kind, w, x_buf.at[w, b_mine], rb3.at[s], yp)
        if kind == "B4":
            return rc(kind, w, fin.at[w, b_mine], fin.at[w, b_mine], zm)
        if kind == "B5a":
            return rc(kind, w, fin.at[w, b_mine], fin.at[w, b_mine], zp)
        if kind == "B5b":
            return rc(kind, w, fin.at[w, b_other], fin.at[w, b_other], zp)
        if kind == "G":
            there = red.at[w, pl.ds(pl.multiple_of(c * RW, RW), RW)]
            return rc(kind, w, fin.at[w], there, sib)

    def p_ff(w):
        return rc("P", w, ffg.at[w, pl.ds(pl.multiple_of((1 - c) * RW, RW), RW)], x_buf.at[w], sib)

    def p_at(j):
        return rc("P", n_ff + j, ag.at[2 * j + 1 - c], x_buf.at[n_ff + j], sib)

    def local(w):
        here = red.at[w, pl.ds(pl.multiple_of(c * RW, RW), RW)]
        return pltpu.make_async_copy(fin.at[w], here, loc_sem.at[w])

    def own_copy(w):
        return pltpu.make_async_copy(
            ffg.at[w, pl.ds(pl.multiple_of(c * RW, RW), RW)], own.at[lax.rem(w, 2)], own_sem.at[lax.rem(w, 2)]
        )

    def add(a, b):
        return (a.astype(f32) + b.astype(f32)).astype(bf16)

    def stage(s, t):
        w = t - (s - 1)
        ok = jnp.logical_and(w >= 0, w < waves)
        slot = lax.rem(w, NS)
        if s == 1:

            @pl.when(jnp.logical_and(ok, w < n_ff))
            def _():
                @pl.when(w + 1 < n_ff)
                def _():
                    own_copy(w + 1).start()

                p_ff(w).wait_recv()
                own_copy(w).wait()
                x_buf[w] = add(x_buf[w], own[lax.rem(w, 2)])

            @pl.when(jnp.logical_and(ok, w >= n_ff))
            def _():
                p_at(w - n_ff).wait_recv()
                x_buf[w] = add(x_buf[w], ag[2 * (w - n_ff) + c])

            @pl.when(ok)
            def _():
                cp("A1", w).start()

                @pl.when(outer)
                def _():
                    cp("B1", w).start()

        if s == 2:

            @pl.when(ok)
            def _():
                cp("A1", w).wait_recv()
                x_buf[w, a_mine] = add(x_buf[w, a_mine], ra1[slot])

                @pl.when(outer)
                def _():
                    cp("A2", w).start()

                @pl.when(inner)
                def _():
                    cp("B1", w).wait_recv()
                    x_buf[w, b_all] = add(x_buf[w, b_all], rb1[slot])
                    cp("B2", w).start()

        if s == 3:

            @pl.when(jnp.logical_and(ok, inner))
            def _():
                cp("A2", w).wait_recv()
                x_buf[w, a_mine] = add(x_buf[w, a_mine], ra2[slot])
                cp("A3", w).start()
                cp("B2", w).wait_recv()
                x_buf[w, b_mine] = add(x_buf[w, b_mine], rb2[slot])
                cp("B3", w).start()

        if s == 4:

            @pl.when(jnp.logical_and(ok, inner))
            def _():
                cp("A3", w).wait_recv()
                fin[w, a_mine] = add(x_buf[w, a_mine], ra3[slot])
                cp("A4", w).start()
                cp("A5", w).start()
                cp("B3", w).wait_recv()
                fin[w, b_mine] = add(x_buf[w, b_mine], rb3[slot])
                cp("B4", w).start()
                cp("B5a", w).start()

        if s == 5:

            @pl.when(jnp.logical_and(ok, inner))
            def _():
                cp("B4", w).wait_recv()
                cp("B5b", w).start()

            @pl.when(jnp.logical_and(ok, outer))
            def _():
                cp("A4", w).wait_recv()
                cp("A5", w).start()

        if s == 6:

            @pl.when(ok)
            def _():
                cp("A5", w).wait_recv()

                @pl.when(outer)
                def _():
                    cp("B5a", w).wait_recv()
                    cp("B5b", w).wait_recv()

                cp("G", w).start()
                local(w).start()


    cos, sin = cs[0:8], cs[8:16]

    def head(t):
        qr = pl.ds(pl.multiple_of(t * 192, 64), 192)
        vr = pl.ds(pl.multiple_of(t * 64, 64), 64)
        qkv_s[...] = dot_nt(w_t[qr], h[...]) + bq[qr]
        do_s[...] = dot_nt(wo[vr], g[...]).astype(bf16)
        o, dq, dk, dv = attend_head(qkv_s[0:64], qkv_s[64:128], qkv_s[128:192], do_s[...], cos, sin)
        att_t[vr] = o
        dqkv_t[pl.ds(pl.multiple_of(t * 192, 64), 64)] = dq.astype(bf16)
        dqkv_t[pl.ds(pl.multiple_of(t * 192 + 64, 64), 64)] = dk.astype(bf16)
        dqkv_t[pl.ds(pl.multiple_of(t * 192 + 128, 64), 64)] = dv.astype(bf16)
        ag[t, 0:192] = dot(dqkv_t[qr], h[...]).astype(bf16)
        ag[t, 192:256] = dot(att_t[vr], g[...]).astype(bf16)

    ch = 128
    n_ch = out.shape[0] // ch

    def xcopy(which, i):
        src, dst = ((br_send, br_recv), (dh_send, dh_recv))[which]
        r = pl.ds(pl.multiple_of(i * ch, ch), ch)
        return pltpu.make_async_remote_copy(
            src_ref=src.at[r], dst_ref=dst.at[r], send_sem=x_ss.at[which, i], recv_sem=x_rs.at[which, i],
            device_id=xp, device_id_type=MESH,
        )

    def load(src, row, buf, sem):
        k = pltpu.make_async_copy(src.at[pl.ds(row, ch)], buf, sem)
        k.start()
        k.wait()

    def norm(i):
        r = resid[i].astype(f32)
        centered = r - jnp.mean(r, axis=1, keepdims=True)
        inv = lax.rsqrt(jnp.mean(centered * centered, axis=1, keepdims=True) + epsilon)
        return r, centered * inv, inv

    def rows_of(who, i):
        return pl.multiple_of(who * (n_ch * ch) + i * ch, ch)

    def branch(row):
        return dot(att_t[:, pl.ds(row, ch)].T, wo[...])

    def back(row):
        return dot(dqkv_t[:, pl.ds(row, ch)].T, w_t[...])

    def add_sums(d, row):
        _, normed, _ = norm(pl.ds(row, ch))
        sums[0:1] = sums[0:1] + jnp.sum(d * normed, axis=0, keepdims=True)
        sums[1:2] = sums[1:2] + jnp.sum(d, axis=0, keepdims=True)

    def branch_far(i, _):
        row = rows_of(1 - x, i)
        load(ffb, row, ff_buf, ff_sem.at[0])
        br_send[pl.ds(pl.multiple_of(i * ch, ch), ch)] = (branch(row) + ff_buf[...]).astype(bf16)
        xcopy(0, i).start()
        return 0

    def back_far(i, _):
        row = rows_of(1 - x, i)
        load(ffd, row, ff_buf, ff_sem.at[0])
        d = back(row) + ff_buf[...]
        add_sums(d, row)
        dh_send[pl.ds(pl.multiple_of(i * ch, ch), ch)] = d.astype(bf16)
        xcopy(1, i).start()
        return 0

    def back_near(i, _):
        row = rows_of(x, i)
        load(ffd, row, ff_buf, ff_sem.at[0])
        d = back(row) + ff_buf[...]
        add_sums(d, row)
        dh_own[pl.ds(pl.multiple_of(i * ch, ch), ch)] = d
        return 0

    def branch_near(i, _):
        row = rows_of(x, i)
        here = pl.ds(pl.multiple_of(i * ch, ch), ch)
        load(ffb, row, ff_buf, ff_sem.at[0])
        xcopy(0, i).wait_recv()
        total = branch(row) + ff_buf[...] + br_recv[here].astype(f32)
        out[here] = (resid[pl.ds(row, ch)].astype(f32) + total + vecs[1:2]).astype(bf16)
        return 0

    def finish(i, _):
        row = rows_of(x, i)
        here = pl.ds(pl.multiple_of(i * ch, ch), ch)
        xcopy(1, i).wait_recv()
        _, normed, inv = norm(pl.ds(row, ch))
        d_hat = (dh_own[here] + dh_recv[here].astype(f32)) * vecs[0:1]
        first = jnp.mean(d_hat, axis=1, keepdims=True)
        second = jnp.mean(d_hat * normed, axis=1, keepdims=True)
        grad_in[here] = g[pl.ds(row, ch)].astype(f32) + inv * (d_hat - first - normed * second)
        return 0

    def small(i):
        device = (sib, yp, zp, zm, xp)[i]
        return pltpu.make_async_remote_copy(
            src_ref=sm_send.at[i], dst_ref=sm_recv.at[i], send_sem=sm_ss.at[i], recv_sem=sm_rs.at[i],
            device_id=device, device_id_type=MESH,
        )


    def start_ff(w, _):
        p_ff(w).start()
        return 0

    own_copy(0).start()
    lax.fori_loop(0, n_ff, start_ff, 0)
    sums[...] = jnp.zeros_like(sums)

    def tick(t, _):
        for s in range(1, 7):
            stage(s, t)

        @pl.when(t < heads)
        def _():
            head(t)

            @pl.when(lax.rem(t, 2) == 1)
            def _():
                p_at(t // 2).start()

        at = lambda k: pl.when(t == heads + k)

        @at(0)
        def _():
            lax.fori_loop(0, n_ch, branch_far, 0)

        @at(1)
        def _():
            lax.fori_loop(0, n_ch, back_far, 0)

        @at(2)
        def _():
            lax.fori_loop(0, n_ch, back_near, 0)
            ones = jnp.ones((8, dqkv_t.shape[1]), bf16)
            bias = dot_nt(ones, dqkv_t[...])
            sm_send[0] = small_in[...]
            wide = small_in.shape[1]
            sm_send[0, 3:4] = bias[0:1, :wide]
            sm_send[0, 4:5, 0 : bias.shape[1] - wide] = bias[0:1, wide:]
            sm_send[0, 5:7] = sums[0:2]
            small(0).start()

        @at(3)
        def _():
            lax.fori_loop(0, n_ch, branch_near, 0)

        for k in range(1, 6):

            @at(2 + k)
            def _():
                small(k - 1).wait_recv()
                total = sm_send[k - 1] + sm_recv[k - 1]
                if k < 4:
                    sm_send[k] = total
                    small(k).start()
                elif k == 4:
                    small_out[...] = total
                    sm_send[4] = total
                    small(4).start()
                else:
                    small_out[5:7] = total[5:7]

        @at(8)
        def _():
            lax.fori_loop(0, n_ch, finish, 0)

        return 0

    lax.fori_loop(0, waves + 5, tick, 0)

    def drain(w, _):
        cp("A1", w).wait_send()
        cp("A5", w).wait_send()
        cp("G", w).wait()
        local(w).wait()

        @pl.when(outer)
        def _():
            cp("B1", w).wait_send()
            cp("A2", w).wait_send()

        @pl.when(inner)
        def _():
            for k in ("B2", "A3", "B3", "A4", "B4", "B5a", "B5b"):
                cp(k, w).wait_send()

        @pl.when(w < n_ff)
        def _():
            p_ff(w).wait_send()

        @pl.when(w >= n_ff)
        def _():
            p_at(w - n_ff).wait_send()

        return 0

    lax.fori_loop(0, waves, drain, 0)

    def drain_x(i, _):
        xcopy(0, i).wait_send()
        xcopy(1, i).wait_send()
        return 0

    lax.fori_loop(0, n_ch, drain_x, 0)
    for i in range(5):
        small(i).wait_send()


def mega(ffg, h, g, w_t, bq, wo, cs, ffb, ffd, resid, vecs, small_in):
    rows, width = h.shape
    heads = wo.shape[0] // HD
    n_ff = ffg.shape[0]
    waves = n_ff + heads // 2
    half = rows // 2
    n_ch = half // 128
    vm = pl.BlockSpec(memory_space=pltpu.VMEM)
    hbm = pl.BlockSpec(memory_space=pl.ANY)
    dma = pltpu.SemaphoreType.DMA
    return pl.pallas_call(
        functools.partial(mega_kernel, n_ff, heads),
        in_specs=[hbm, vm, vm, vm, vm, vm, vm, hbm, hbm, vm, vm, vm],
        out_specs=[hbm, vm, vm, vm],
        out_shape=[
            jax.ShapeDtypeStruct((waves, 2 * RW, width), bf16),
            jax.ShapeDtypeStruct((half, width), bf16),
            jax.ShapeDtypeStruct((half, width), f32),
            jax.ShapeDtypeStruct((8, width), f32),
        ],
        scratch_shapes=[
            pltpu.VMEM((waves, RW, width), bf16),
            pltpu.VMEM((2, RW, width), bf16),
            pltpu.VMEM((heads, RW, width), bf16),
            pltpu.VMEM((waves, RW, width), bf16),
            pltpu.VMEM((NS, RQ, width), bf16),
            pltpu.VMEM((NS, RQ, width), bf16),
            pltpu.VMEM((NS, RQ, width), bf16),
            pltpu.VMEM((NS, 2 * RQ, width), bf16),
            pltpu.VMEM((NS, RQ, width), bf16),
            pltpu.VMEM((NS, RQ, width), bf16),
            pltpu.VMEM((3 * HD, rows), f32),
            pltpu.VMEM((HD, rows), bf16),
            pltpu.VMEM((heads * 3 * HD, rows), bf16),
            pltpu.VMEM((heads * HD, rows), bf16),
            pltpu.VMEM((half, width), f32),
            pltpu.VMEM((half, width), bf16),
            pltpu.VMEM((half, width), bf16),
            pltpu.VMEM((half, width), bf16),
            pltpu.VMEM((half, width), bf16),
            pltpu.VMEM((128, width), f32),
            pltpu.VMEM((8, width), f32),
            pltpu.VMEM((5, 8, width), f32),
            pltpu.VMEM((5, 8, width), f32),
            pltpu.VMEM((8, width), f32),
            dma((len(KINDS), waves)),
            dma((len(KINDS), waves)),
            dma((2,)),
            dma((waves,)),
            dma((2, n_ch)),
            dma((2, n_ch)),
            dma((2,)),
            dma((5,)),
            dma((5,)),
            dma((2,)),
        ],
        compiler_params=pltpu.CompilerParams(collective_id=0, has_side_effects=True, vmem_limit_bytes=62 * 2**20),
        name="attention_and_sums",
    )(ffg, h, g, w_t, bq, wo, cs, ffb, ffd, resid, vecs, small_in)


def shards(residual, ln_gain, ln_bias, w_qkv, b_qkv, w_out, b_out, w_up, b_up, w_down, b_down, grad_out):
    x = lax.axis_index("tensor")
    swap = [(0, 1), (1, 0)]
    far_resid = lax.ppermute(residual, "tensor", swap)
    grad_first, far_resid = lax.optimization_barrier((grad_out, far_resid))
    far_grad = lax.ppermute(grad_first, "tensor", swap)

    def group(near, far):
        return jnp.where(x == 0, jnp.concatenate([near, far]), jnp.concatenate([far, near]))

    resid = group(residual, far_resid)
    wide = resid.astype(f32)
    centered = wide - jnp.mean(wide, axis=1, keepdims=True)
    variance = jnp.mean(centered * centered, axis=1, keepdims=True)
    normed = centered * lax.rsqrt(variance + epsilon)
    h = (normed * ln_gain + ln_bias).astype(bf16)
    g = group(grad_out, far_grad)
    up_lin = dot(h, w_up) + b_up
    act_wide, gelu_back = jax.vjp(functools.partial(jax.nn.gelu, approximate=False), up_lin)
    slope = gelu_back(jnp.ones_like(up_lin))[0].astype(bf16)
    act = act_wide.astype(bf16)
    act, slope = lax.optimization_barrier((act, slope))
    ffb = dot(act, w_down)
    d_up = (dot_nt(g, w_down) * slope.astype(f32)).astype(bf16)
    ffd = dot_nt(d_up, w_up)
    g_down = dot_tn(act, g).astype(bf16)
    g_up = dot_tn(h, d_up).astype(bf16)
    rows, width = h.shape
    n_up = g_up.shape[1] // width
    blocks = [g_down.reshape(-1, 2 * RW, width)]
    blocks += [g_up[:, i * width : (i + 1) * width].reshape(-1, 2 * RW, width) for i in range(n_up)]
    ffg = jnp.concatenate(blocks)
    n_down = blocks[0].shape[0]
    gb_up = jnp.sum(d_up, axis=0, dtype=f32)
    gb_near = jnp.sum(grad_out, axis=0, dtype=f32)
    gb_far = jnp.sum(far_grad, axis=0, dtype=f32)
    gb_out = gb_near + gb_far
    small_in = jnp.concatenate([gb_up.reshape(n_up, width), gb_out[None], jnp.zeros((7 - n_up, width), f32)])
    cosine, sine = turn_tables(rows)
    cs = jnp.concatenate([cosine.T, sine.T])
    vecs = jnp.concatenate([ln_gain[None], (b_out + b_down)[None], jnp.zeros((6, width), f32)])
    red, out, grad_in, small = mega(ffg, h, g, w_qkv.T, b_qkv[:, None], w_out, cs, ffb, ffd, resid, vecs, small_in)
    grad_w_down = red[:n_down].reshape(-1, width).astype(f32)
    per = width // (2 * RW)
    ups = [red[n_down + i * per : n_down + (i + 1) * per].reshape(width, width) for i in range(n_up)]
    grad_w_up = jnp.concatenate(ups, axis=1).astype(f32)
    at = red[n_down + n_up * per :].reshape(-1, RW, width)
    grad_w_qkv = at[:, : 3 * HD].reshape(-1, width).T.astype(f32)
    grad_w_out = at[:, 3 * HD :].reshape(-1, width).astype(f32)
    gb_up = small[:n_up].reshape(-1)
    gb_out = small[2]
    gb_qkv = small[3:5].reshape(-1)[: b_qkv.shape[0]]
    return out, grad_in, small[5], small[6], grad_w_qkv, gb_qkv, grad_w_out, gb_out, grad_w_up, gb_up, grad_w_down, gb_out


def contract_rows(left, right):
    return lax.dot_general(
        left, right, (((0,), (0,)), ((), ())), preferred_element_type=jnp.float32
    )


def contract_cols(left, right):
    return lax.dot_general(
        left, right, (((1,), (1,)), ((), ())), preferred_element_type=jnp.float32
    )


def turn_heads(heads, cosine, sine):
    half_rot = ROT // 2
    first = heads[:, :, :half_rot]
    second = heads[:, :, half_rot:ROT]
    rest = heads[:, :, ROT:]
    cos_rows = cosine[:, None, :]
    sin_rows = sine[:, None, :]
    return jnp.concatenate(
        [first * cos_rows - second * sin_rows, second * cos_rows + first * sin_rows, rest], axis=2
    )


def undo_turn(heads, cosine, sine):
    half_rot = ROT // 2
    first = heads[:, :, :half_rot]
    second = heads[:, :, half_rot:ROT]
    rest = heads[:, :, ROT:]
    cos_rows = cosine[:, None, :]
    sin_rows = sine[:, None, :]
    return jnp.concatenate(
        [first * cos_rows + second * sin_rows, second * cos_rows - first * sin_rows, rest], axis=2
    )


def shards_any(
    residual, ln_gain, ln_bias, w_qkv, b_qkv, w_out, b_out, w_up, b_up, w_down, b_down, grad_out
):
    rows_here = residual.shape[0]
    head_cols = w_out.shape[0]
    heads_here = head_cols // HD
    resid_wide = residual.astype(jnp.float32)
    average = jnp.mean(resid_wide, axis=1, keepdims=True)
    centered = resid_wide - average
    variance = jnp.mean(centered * centered, axis=1, keepdims=True)
    inv_std = lax.rsqrt(variance + epsilon)
    normed = centered * inv_std
    h_local = (normed * ln_gain + ln_bias).astype(jnp.bfloat16)
    h_full = lax.all_gather(h_local, "tensor", axis=0, tiled=True)
    group_rows = h_full.shape[0]
    seqlen = min(LEN_MAX, group_rows)
    seq_count = group_rows // seqlen
    qkv = jnp.dot(h_full, w_qkv, preferred_element_type=jnp.float32) + b_qkv
    up_lin = jnp.dot(h_full, w_up, preferred_element_type=jnp.float32) + b_up
    act_wide, gelu_back = jax.vjp(functools.partial(jax.nn.gelu, approximate=False), up_lin)
    act = act_wide.astype(jnp.bfloat16)
    cosine, sine = turn_tables(seqlen)
    causal = jnp.arange(seqlen)[:, None] >= jnp.arange(seqlen)[None, :]
    scale = 1.0 / math.sqrt(HD)

    def attend(block):
        queries = turn_heads(block[:, :, 0, :], cosine, sine).astype(jnp.bfloat16)
        key_rows = turn_heads(block[:, :, 1, :], cosine, sine).astype(jnp.bfloat16)
        value_rows = block[:, :, 2, :].astype(jnp.bfloat16)
        scores = (
            jnp.einsum("qhd,khd->hqk", queries, key_rows, preferred_element_type=jnp.float32)
            * scale
        )
        scores = jnp.where(causal[None], scores, -1e30)
        peak = jnp.max(scores, axis=2, keepdims=True)
        raised = jnp.exp(scores - peak)
        totals = jnp.sum(raised, axis=2, keepdims=True)
        probs = raised / totals
        attended = jnp.einsum(
            "hqk,khd->qhd",
            probs.astype(jnp.bfloat16),
            value_rows,
            preferred_element_type=jnp.float32,
        ).astype(jnp.bfloat16)
        log_total = peak[:, :, 0] + jnp.log(totals[:, :, 0])
        return (queries, key_rows, value_rows, attended, log_total)

    blocks = qkv.reshape(seq_count, seqlen, heads_here, 3, HD)
    queries, key_rows, value_rows, attended, log_total = lax.map(attend, blocks)
    attn_rows = attended.reshape(group_rows, head_cols)
    act_part = lax.slice_in_dim(act, 0, lax.axis_size("tensor") * rows_here, axis=0)
    branch = lax.psum_scatter(
        jnp.dot(attn_rows, w_out, preferred_element_type=jnp.float32)
        + jnp.dot(act_part, w_down, preferred_element_type=jnp.float32),
        "tensor",
        scatter_dimension=0,
        tiled=True,
    )
    out = (resid_wide + branch + b_out + b_down).astype(jnp.bfloat16)
    grad_local = grad_out.astype(jnp.float32)
    grad_full = lax.all_gather(grad_out, "tensor", axis=0, tiled=True)
    grad_w_out = contract_rows(attn_rows, grad_full)
    grad_w_down = contract_rows(act, grad_full)
    d_attended = contract_cols(grad_full, w_out).astype(jnp.bfloat16)
    d_act = contract_cols(grad_full, w_down)
    d_up = gelu_back(d_act)[0].astype(jnp.bfloat16)
    grad_b_up = jnp.sum(d_up, axis=0, dtype=jnp.float32)

    def attend_back(items):
        query_part, key_part, value_part, log_part, d_part = items
        scores = (
            jnp.einsum("qhd,khd->hqk", query_part, key_part, preferred_element_type=jnp.float32)
            * scale
        )
        probs = jnp.where(causal[None], jnp.exp(scores - log_part[:, :, None]), 0.0)
        grad_values = jnp.einsum(
            "hqk,qhd->khd", probs.astype(jnp.bfloat16), d_part, preferred_element_type=jnp.float32
        )
        d_probs = jnp.einsum("qhd,khd->hqk", d_part, value_part, preferred_element_type=jnp.float32)
        d_scores = (probs * (d_probs - jnp.sum(d_probs * probs, axis=2, keepdims=True))).astype(
            jnp.bfloat16
        )
        d_query = (
            jnp.einsum("hqk,khd->qhd", d_scores, key_part, preferred_element_type=jnp.float32)
            * scale
        )
        d_key = (
            jnp.einsum("hqk,qhd->khd", d_scores, query_part, preferred_element_type=jnp.float32)
            * scale
        )
        return jnp.stack(
            [undo_turn(d_query, cosine, sine), undo_turn(d_key, cosine, sine), grad_values], axis=2
        )

    d_blocks = d_attended.reshape(seq_count, seqlen, heads_here, HD)
    d_qkv = lax.map(attend_back, (queries, key_rows, value_rows, log_total, d_blocks))
    d_qkv = d_qkv.reshape(group_rows, 3 * head_cols).astype(jnp.bfloat16)
    grad_b_qkv = jnp.sum(d_qkv, axis=0, dtype=jnp.float32)
    grad_w_qkv = contract_rows(h_full, d_qkv)
    grad_w_up = contract_rows(h_full, d_up)
    d_hidden = lax.psum_scatter(
        contract_cols(d_qkv, w_qkv) + contract_cols(d_up, w_up),
        "tensor",
        scatter_dimension=0,
        tiled=True,
    )
    gain_local = jnp.sum(d_hidden * normed, axis=0)
    bias_local = jnp.sum(d_hidden, axis=0)
    d_hat = d_hidden * ln_gain
    grad_in = grad_local + inv_std * (
        d_hat
        - jnp.mean(d_hat, axis=1, keepdims=True)
        - normed * jnp.mean(d_hat * normed, axis=1, keepdims=True)
    )
    out_bias = jnp.sum(grad_full, axis=0, dtype=jnp.float32)
    grad_w_qkv, grad_b_qkv, grad_w_out, grad_w_up, grad_b_up, grad_w_down, grad_b_out = lax.psum(
        (grad_w_qkv, grad_b_qkv, grad_w_out, grad_w_up, grad_b_up, grad_w_down, out_bias), "dp"
    )
    grad_ln_gain, grad_ln_bias = lax.psum((gain_local, bias_local), ("dp", "tensor"))
    return (
        out,
        grad_in,
        grad_ln_gain,
        grad_ln_bias,
        grad_w_qkv,
        grad_b_qkv,
        grad_w_out,
        grad_b_out,
        grad_w_up,
        grad_b_up,
        grad_w_down,
        grad_b_out,
    )


def solution(mesh):
    small_slice = mesh.shape["dp"] == 16 and mesh.shape["tensor"] == 2
    return jax.shard_map(
        shards if small_slice else shards_any,
        mesh=mesh,
        in_specs=(
            P(("dp", "tensor"), None),
            P(),
            P(),
            P(None, "tensor"),
            P("tensor"),
            P("tensor", None),
            P(),
            P(None, "tensor"),
            P("tensor"),
            P("tensor", None),
            P(),
            P(("dp", "tensor"), None),
        ),
        out_specs=(
            P(("dp", "tensor"), None),
            P(("dp", "tensor"), None),
            P(),
            P(),
            P(None, "tensor"),
            P("tensor"),
            P("tensor", None),
            P(),
            P(None, "tensor"),
            P("tensor"),
            P("tensor", None),
            P(),
        ),
        check_vma=False,
    )
```

```python
import functools
import math

import jax
import jax.numpy as jnp
from jax import lax
from jax.experimental import pallas as pl
from jax.experimental.pallas import tpu as pltpu
from jax.sharding import PartitionSpec as P

HD = 64
ROT = 16
LEN_MAX = 1024
epsilon = 1e-05
MESH = pl.DeviceIdType.MESH
f32 = jnp.float32
bf16 = jnp.bfloat16


def dot(left, right):
    return lax.dot_general(left, right, (((1,), (0,)), ((), ())), preferred_element_type=f32)


def dot_nt(left, right):
    return lax.dot_general(left, right, (((1,), (1,)), ((), ())), preferred_element_type=f32)


def turn_tables(seqlen):
    half_rot = ROT // 2
    exponent = jnp.arange(half_rot, dtype=f32) * (2.0 / ROT)
    inverse = 1.0 / 10000.0**exponent
    places = jnp.arange(seqlen, dtype=f32)
    angles = places[:, None] * inverse[None, :]
    return (jnp.cos(angles), jnp.sin(angles))


def turn(t, cos, sin, sign):
    a, b = t[0:8], t[8:16]
    return jnp.concatenate([a * cos - sign * (b * sin), b * cos + sign * (a * sin), t[16:]], axis=0)


def attend_head(q_t, k_t, v_t, do_t, cos, sin, blk=256):
    seq = q_t.shape[1]
    nb = seq // blk
    qs = turn(q_t, cos, sin, 1.0).astype(bf16) * jnp.asarray(0.125, bf16)
    kb = turn(k_t, cos, sin, 1.0).astype(bf16)
    vb = v_t.astype(bf16)
    keys, values, queries, grads = kb.T, vb.T, qs.T, do_t.T
    seen = lax.broadcasted_iota(jnp.int32, (blk, blk), 0) <= lax.broadcasted_iota(jnp.int32, (blk, blk), 1)
    outs, dqs, dv_sum, dk_sum = [], [], [None] * nb, [None] * nb

    def products(i):
        kk, sl = (i + 1) * blk, slice(i * blk, (i + 1) * blk)
        return dot(keys[:kk], qs[:, sl]), dot(values[:kk], do_t[:, sl])

    def gather(sums, i, v):
        for j in range(i + 1):
            a = v[j * blk : (j + 1) * blk]
            sums[j] = a if sums[j] is None else sums[j] + a

    def back(i, p, dp):
        kk, sl = (i + 1) * blk, slice(i * blk, (i + 1) * blk)
        ds = (p * (dp - jnp.sum(p * dp, axis=0, keepdims=True))).astype(bf16)
        dqs.append(dot(kb[:, :kk], ds) * 0.125)
        gather(dk_sum, i, dot(ds, queries[sl]))

    ahead, behind = products(0), None
    for i in range(nb):
        kk, sl = (i + 1) * blk, slice(i * blk, (i + 1) * blk)
        s, dp = ahead
        if i + 1 < nb:
            ahead = products(i + 1)
        diag = jnp.where(seen, s[i * blk :], -1e30)
        s = jnp.concatenate([s[: i * blk], diag], axis=0) if i else diag
        p = jnp.exp(s - jnp.max(s, axis=0, keepdims=True))
        p = p * (1.0 / jnp.sum(p, axis=0, keepdims=True))
        pb = p.astype(bf16)
        outs.append(dot(vb[:, :kk], pb).astype(bf16))
        gather(dv_sum, i, dot(pb, grads[sl]))
        if behind is not None:
            back(*behind)
        behind = (i, p, dp)
    back(*behind)
    dq_t = turn(jnp.concatenate(dqs, axis=1), cos, sin, -1.0)
    dk_t = turn(jnp.concatenate(dk_sum, axis=0).T, cos, sin, -1.0)
    dv_t = jnp.concatenate(dv_sum, axis=0).T
    return jnp.concatenate(outs, axis=1), dq_t, dk_t, dv_t


def gelu_and_slope(u):
    half = 0.5 + 0.5 * lax.erf(u * (1.0 / math.sqrt(2.0)))
    bell = jnp.exp(u * u * -0.5) * (1.0 / math.sqrt(2.0 * math.pi))
    return u * half, half + u * bell


RW = 256
RQ = RW // 4
NS = 4
NP = 2
KINDS = ("P", "A1", "A2", "A3", "A4", "A5", "B1", "B2", "B3", "B4", "B5a", "B5b", "G")
KI = {k: i for i, k in enumerate(KINDS)}
HEAD_TICKS = (2, 4, 5, 6, 7, 8, 8, 9)
LATE = HEAD_TICKS[-1] + 1
BC = 512
WC = 256
N_LOADS = 3


def mega_kernel(
    heads,
    g_n, r_n, w_qkv, wo, w_up, w_down, bq, bu, cs, ln_gain, ln_bias, b_out, b_down,
    red, out, grad_in, small_out,
    act2, dup2, h2, g2, r2, w_t2, wo2, x_buf, fw, ag, fin, ra1, ra2, ra3, rb1, rb2, rb3,
    qkv_s, do_s, dqkv_t, att_t, t_buf, bq_s, acc, acc2, wd, wu,
    sm_send, sm_recv, sums,
    ss, rs, loc_sem, load_sem, r_ss, r_rs, g_ss, g_rs, x_ss, x_rs, wd_sem, wu_sem, sm_ss, sm_rs, out_sem, free_sem,
):
    half, width = g_n.shape
    hidden = w_down.shape[0]
    n_g = width // RW
    n_ff = n_g + n_g
    n_at = heads // 2
    waves = n_ff + n_at
    dp, x = lax.axis_index("dp"), lax.axis_index("tensor")
    c, y, z = lax.rem(dp, 2), lax.rem(dp // 2, 2), dp // 4
    dev = lambda zz, yy, cc, xx: (zz * 4 + yy * 2 + cc, xx)
    sib = dev(z, y, 1 - c, x)
    yp = dev(z, 1 - y, c, x)
    zp = dev(z + 1 - 2 * lax.rem(z, 2), y, c, x)
    zm = dev(3 - z, y, c, x)
    xp = dev(z, y, c, 1 - x)
    inner = jnp.logical_or(z == 1, z == 2)
    outer = jnp.logical_not(inner)
    near = pl.ds(pl.multiple_of(x * half, half), half)
    far = pl.ds(pl.multiple_of((1 - x) * half, half), half)

    loads = []
    for src, dst in ((r_n, r2.at[near]), (g_n, g2.at[near]), (wo, wo2)):
        loads.append(pltpu.make_async_copy(src, dst, load_sem.at[len(loads)]))
    for k in loads:
        k.start()

    barrier = pltpu.get_barrier_semaphore()
    for d in (xp, sib, yp, zp, zm):
        pl.semaphore_signal(barrier, inc=1, device_id=d, device_id_type=MESH)
    pl.semaphore_wait(barrier, 5)

    def g_copy(i):
        cols = pl.ds(pl.multiple_of(i * RW, RW), RW)
        return pltpu.make_async_remote_copy(
            src_ref=g_n.at[:, cols], dst_ref=g2.at[near, cols], send_sem=g_ss.at[i], recv_sem=g_rs.at[i],
            device_id=xp, device_id_type=MESH,
        )

    def g_arrives(i):
        cols = pl.ds(pl.multiple_of(i * RW, RW), RW)
        pltpu.make_async_remote_copy(
            src_ref=g_n.at[:, cols], dst_ref=g2.at[far, cols], send_sem=g_ss.at[i], recv_sem=g_rs.at[i],
            device_id=xp, device_id_type=MESH,
        ).wait_recv()

    rb = 256
    n_rb = half // rb

    def rows_of(who, i):
        return pl.ds(pl.multiple_of(who * half + i * rb, rb), rb)

    def r_copy(i, who):
        return pltpu.make_async_remote_copy(
            src_ref=r_n.at[pl.ds(pl.multiple_of(i * rb, rb), rb)], dst_ref=r2.at[rows_of(who, i)],
            send_sem=r_ss.at[i], recv_sem=r_rs.at[i], device_id=xp, device_id_type=MESH,
        )

    for i in range(n_rb):
        r_copy(i, x).start()


    a_mine = pl.ds(pl.multiple_of(y * RQ, RQ), RQ)
    a_other = pl.ds(pl.multiple_of((1 - y) * RQ, RQ), RQ)
    zi = jnp.where(z == 2, 1, 0)
    b_mine = pl.ds(pl.multiple_of(2 * RQ + zi * RQ, RQ), RQ)
    b_other = pl.ds(pl.multiple_of(2 * RQ + (1 - zi) * RQ, RQ), RQ)
    b_all = pl.ds(2 * RQ, 2 * RQ)

    def rc(kind, w, src, dst, device):
        k = KI[kind]
        return pltpu.make_async_remote_copy(
            src_ref=src, dst_ref=dst, send_sem=ss.at[k, w], recv_sem=rs.at[k, w], device_id=device, device_id_type=MESH
        )

    def cp(kind, w):
        s = lax.rem(w, NS)
        if kind == "A1":
            return rc(kind, w, x_buf.at[w, a_other], ra1.at[s], yp)
        if kind == "A2":
            return rc(kind, w, x_buf.at[w, a_mine], ra2.at[s], zp)
        if kind == "A3":
            return rc(kind, w, x_buf.at[w, a_mine], ra3.at[s], zm)
        if kind == "A4":
            return rc(kind, w, fin.at[w, a_mine], fin.at[w, a_mine], zp)
        if kind == "A5":
            return rc(kind, w, fin.at[w, a_mine], fin.at[w, a_mine], yp)
        if kind == "B1":
            return rc(kind, w, x_buf.at[w, b_all], rb1.at[s], zp)
        if kind == "B2":
            return rc(kind, w, x_buf.at[w, b_other], rb2.at[s], zm)
        if kind == "B3":
            return rc(kind, w, x_buf.at[w, b_mine], rb3.at[s], yp)
        if kind == "B4":
            return rc(kind, w, fin.at[w, b_mine], fin.at[w, b_mine], zm)
        if kind == "B5a":
            return rc(kind, w, fin.at[w, b_mine], fin.at[w, b_mine], zp)
        if kind == "B5b":
            return rc(kind, w, fin.at[w, b_other], fin.at[w, b_other], zp)
        if kind == "G":
            there = red.at[w, pl.ds(pl.multiple_of(c * RW, RW), RW)]
            return rc(kind, w, fin.at[w], there, sib)

    def p_ff(w):
        return rc("P", w, fw.at[lax.rem(w, 2), 1 - c], x_buf.at[w], sib)

    def p_at(j):
        return rc("P", n_ff + j, ag.at[lax.rem(j, NP), 1 - c], x_buf.at[n_ff + j], sib)

    def local(w):
        here = red.at[w, pl.ds(pl.multiple_of(c * RW, RW), RW)]
        return pltpu.make_async_copy(fin.at[w], here, loc_sem.at[w])

    def add(a, b):
        return (a.astype(f32) + b.astype(f32)).astype(bf16)

    def stage(s, t):
        w = t - (s - 1)
        ok = jnp.logical_and(w >= 0, w < waves)
        slot = lax.rem(w, NS)
        if s == 1:

            @pl.when(jnp.logical_and(ok, w < n_ff))
            def _():
                p_ff(w).wait_recv()
                x_buf[w] = add(x_buf[w], fw[lax.rem(w, 2), c])

            @pl.when(jnp.logical_and(ok, w >= n_ff))
            def _():
                p_at(w - n_ff).wait_recv()
                x_buf[w] = add(x_buf[w], ag[lax.rem(w - n_ff, NP), c])

            @pl.when(ok)
            def _():
                cp("A1", w).start()

                @pl.when(outer)
                def _():
                    cp("B1", w).start()

        if s == 2:

            @pl.when(ok)
            def _():
                cp("A1", w).wait_recv()
                x_buf[w, a_mine] = add(x_buf[w, a_mine], ra1[slot])

                @pl.when(outer)
                def _():
                    cp("A2", w).start()

                @pl.when(inner)
                def _():
                    cp("B1", w).wait_recv()
                    x_buf[w, b_all] = add(x_buf[w, b_all], rb1[slot])
                    cp("B2", w).start()

        if s == 3:

            @pl.when(jnp.logical_and(ok, inner))
            def _():
                cp("A2", w).wait_recv()
                x_buf[w, a_mine] = add(x_buf[w, a_mine], ra2[slot])
                cp("A3", w).start()
                cp("B2", w).wait_recv()
                x_buf[w, b_mine] = add(x_buf[w, b_mine], rb2[slot])
                cp("B3", w).start()

        if s == 4:

            @pl.when(jnp.logical_and(ok, inner))
            def _():
                cp("A3", w).wait_recv()
                fin[w, a_mine] = add(x_buf[w, a_mine], ra3[slot])
                cp("A4", w).start()
                cp("A5", w).start()
                cp("B3", w).wait_recv()
                fin[w, b_mine] = add(x_buf[w, b_mine], rb3[slot])
                cp("B4", w).start()
                cp("B5a", w).start()

        if s == 5:

            @pl.when(jnp.logical_and(ok, inner))
            def _():
                cp("B4", w).wait_recv()
                cp("B5b", w).start()

            @pl.when(jnp.logical_and(ok, outer))
            def _():
                cp("A4", w).wait_recv()
                cp("A5", w).start()

        if s == 6:

            @pl.when(ok)
            def _():
                cp("A5", w).wait_recv()

                @pl.when(outer)
                def _():
                    cp("B5a", w).wait_recv()
                    cp("B5b", w).wait_recv()

                cp("G", w).start()
                local(w).start()


    def ff_wave(w):
        @pl.when(w >= 2)
        def _():
            p_ff(w - 2).wait_send()

        def product(src, full):
            t_buf[...] = src.T

            def block(n, _):
                cols = pl.ds(pl.multiple_of(n * BC, BC), BC)
                per = width // BC
                fw[lax.rem(w, 2), n // per, :, pl.ds(pl.multiple_of(lax.rem(n, per) * BC, BC), BC)] = dot(
                    t_buf[...], full[:, cols]
                ).astype(bf16)
                return 0

            lax.fori_loop(0, hidden // BC, block, 0)

        @pl.when(w < n_g)
        def _():
            g_arrives(w)
            product(g2[:, pl.ds(pl.multiple_of(w * RW, RW), RW)], act2)

        @pl.when(w >= n_g)
        def _():
            product(h2[:, pl.ds(pl.multiple_of((w - n_g) * RW, RW), RW)], dup2)

        p_ff(w).start()

    def stream(copy, n, body):
        copy(0).start()

        def step(i, _):
            @pl.when(i + 1 < n)
            def _():
                copy(i + 1).start()

            copy(i).wait()
            body(i, lax.rem(i, 2))
            return 0

        lax.fori_loop(0, n, step, 0)

    def wd_copy(i):
        s = lax.rem(i, 2)
        return pltpu.make_async_copy(w_down.at[pl.ds(pl.multiple_of(i * WC, WC), WC)], wd.at[s], wd_sem.at[s])

    def wu_copy(i):
        s = lax.rem(i, 2)
        return pltpu.make_async_copy(w_up.at[:, pl.ds(pl.multiple_of(i * WC, WC), WC)], wu.at[s], wu_sem.at[s])

    def wq_copy(i):
        s = lax.rem(i, 2)
        return pltpu.make_async_copy(w_qkv.at[:, pl.ds(pl.multiple_of(i * WC, WC), WC)], wu.at[s], wu_sem.at[s])

    class both:
        def __init__(self, *copies):
            self.copies = copies

        def start(self):
            for k in self.copies:
                k.start()

        def wait(self):
            for k in self.copies:
                k.wait()

    n_hid = hidden // WC

    def norm(rows):
        r = r2[rows].astype(f32)
        centered = r - jnp.mean(r, axis=1, keepdims=True)
        inv = lax.rsqrt(jnp.mean(centered * centered, axis=1, keepdims=True) + epsilon)
        return r, centered * inv, inv

    def make_hidden(rows):
        h2[rows] = (norm(rows)[1] * ln_gain[...] + ln_bias[...]).astype(bf16)

    def turn_weights():
        def body(n, s):
            w_t2[pl.ds(pl.multiple_of(n * WC, WC), WC)] = wu[s].T

        stream(wq_copy, w_qkv.shape[1] // WC, body)
        for n in range(w_qkv.shape[1] // 128):
            cols = slice(n * 128, (n + 1) * 128)
            bq_s[cols] = jnp.broadcast_to(bq[:, cols], (128, 128)).T

    def ff_near():
        def body(n, s):
            cols = pl.ds(pl.multiple_of(n * WC, WC), WC)

            def block(i, _):
                r = rows_of(x, i)
                a, slope = gelu_and_slope(dot(h2[r], wu[s]) + bu[:, cols])
                act2[r, cols] = a.astype(bf16)
                dup2[r, cols] = (dot_nt(g2[r], wd[s]) * slope).astype(bf16)
                return 0

            lax.fori_loop(0, n_rb, block, 0)

        stream(lambda i: both(wu_copy(i), wd_copy(i)), n_hid, body)

    def ff_far(i):
        r = rows_of(1 - x, i)
        r_copy(i, 1 - x).wait_recv()
        make_hidden(r)

        def body(n, s):
            cols = pl.ds(pl.multiple_of(n * WC, WC), WC)
            a, slope = gelu_and_slope(dot(h2[r], wu[s]) + bu[:, cols])
            act2[r, cols] = a.astype(bf16)
            dup2[r, cols] = slope.astype(bf16)

        stream(wu_copy, n_hid, body)

    def d_up_far():
        def body(n, s):
            cols = pl.ds(pl.multiple_of(n * WC, WC), WC)

            def block(i, _):
                r = rows_of(1 - x, i)
                dup2[r, cols] = (dot_nt(g2[r], wd[s]) * dup2[r, cols].astype(f32)).astype(bf16)
                return 0

            lax.fori_loop(0, n_rb, block, 0)

        stream(wd_copy, n_hid, body)


    cos, sin = cs[0:8], cs[8:16]
    hq, hv = 3 * HD, HD

    def head(t):
        odd = lax.rem(t, 2)
        j = t // 2
        pair_q = pl.ds(pl.multiple_of(j * 2 * hq, 2 * HD), 2 * hq)
        pair_v = pl.ds(pl.multiple_of(j * 2 * hv, 2 * HD), 2 * hv)

        @pl.when(odd == 0)
        def _():
            qkv_s[...] = dot_nt(w_t2[pair_q], h2[...]) + bq_s[pair_q, 0:1]
            do_s[...] = dot_nt(wo2[pair_v], g2[...]).astype(bf16)

        part = lambda i: qkv_s[pl.ds(pl.multiple_of(odd * hq + i * HD, HD), HD)]
        o, dq, dk, dv = attend_head(
            part(0), part(1), part(2), do_s[pl.ds(pl.multiple_of(odd * hv, HD), HD)], cos, sin
        )
        att_t[pl.ds(pl.multiple_of(t * hv, HD), HD)] = o
        for i, v in enumerate((dq, dk, dv)):
            dqkv_t[pl.ds(pl.multiple_of(t * hq + i * HD, HD), HD)] = v.astype(bf16)

        @pl.when(odd == 1)
        def _():
            slot = lax.rem(j, NP)

            @pl.when(j >= NP)
            def _():
                p_at(j - NP).wait_send()

            gq = dot(dqkv_t[pair_q], h2[...]).astype(bf16)
            gv = dot(att_t[pair_v], g2[...]).astype(bf16)
            for i in range(2):
                ag[slot, i, 0:hq] = gq[i * hq : (i + 1) * hq]
                ag[slot, i, hq : hq + hv] = gv[i * hv : (i + 1) * hv]
            p_at(j).start()


    def xcopy(which, i):
        dst = h2
        r = pl.ds(pl.multiple_of(which * half + i * rb, rb), rb)
        return pltpu.make_async_remote_copy(
            src_ref=fw.at[which, i], dst_ref=dst.at[r], send_sem=x_ss.at[which, i], recv_sem=x_rs.at[which, i],
            device_id=xp, device_id_type=MESH,
        )

    def each(body):
        def step(i, _):
            body(i, pl.ds(pl.multiple_of(i * rb, rb), rb))
            return 0

        lax.fori_loop(0, n_rb, step, 0)

    def branch(who, total):
        def start(i, here):
            total[here] = dot(att_t[:, rows_of(who, i)].T, wo2[...])

        each(start)

        def body(n, s):
            cols = pl.ds(pl.multiple_of(n * WC, WC), WC)

            def block(i, here):
                total[here] = total[here] + dot(act2[rows_of(who, i), cols], wd[s])

            each(block)

        stream(wd_copy, n_hid, body)

    def back(who, total):
        def start(i, here):
            total[here] = dot(dqkv_t[:, rows_of(who, i)].T, w_t2[...])

        each(start)

        def body(n, s):
            cols = pl.ds(pl.multiple_of(n * WC, WC), WC)

            def block(i, here):
                total[here] = total[here] + dot_nt(dup2[rows_of(who, i), cols], wu[s])

            each(block)

        stream(wu_copy, n_hid, body)

        def add_sums(i, here):
            _, normed, _ = norm(rows_of(who, i))
            d = total[here]
            sums[0:1] = sums[0:1] + jnp.sum(d * normed, axis=0, keepdims=True)
            sums[1:2] = sums[1:2] + jnp.sum(d, axis=0, keepdims=True)

        each(add_sums)

    def out_copy():
        return pltpu.make_async_copy(h2.at[pl.ds(0, half)], out, out_sem.at[0])

    def branch_far():
        branch(1 - x, acc)
        pl.semaphore_wait(free_sem, 1)

        def send(i, here):
            fw[0, i] = acc[here].astype(bf16)
            xcopy(0, i).start()

        each(send)

    def back_far():
        back(1 - x, acc)

        def send(i, here):
            fw[1, i] = acc[here].astype(bf16)
            xcopy(1, i).start()

        each(send)

    def branch_near():
        for i in range(n_rb):
            r = rows_of(x, i)
            acc2[...] = dot(att_t[:, r].T, wo2[...]) + (b_out[...] + b_down[...])

            def body(n, s):
                cols = pl.ds(pl.multiple_of(n * WC, WC), WC)
                acc2[...] = acc2[...] + dot(act2[r, cols], wd[s])

            stream(wd_copy, n_hid, body)
            xcopy(0, i).wait_recv()
            here = pl.ds(i * rb, rb)
            h2[here] = (r2[r].astype(f32) + acc2[...] + h2[here].astype(f32)).astype(bf16)
        out_copy().start()

    def finish():
        def last(i, here):
            xcopy(1, i).wait_recv()
            _, normed, inv = norm(rows_of(x, i))
            d_hat = (acc[here] + h2[pl.ds(pl.multiple_of(half + i * rb, rb), rb)].astype(f32)) * ln_gain[...]
            first = jnp.mean(d_hat, axis=1, keepdims=True)
            second = jnp.mean(d_hat * normed, axis=1, keepdims=True)
            acc[here] = g2[rows_of(x, i)].astype(f32) + inv * (d_hat - first - normed * second)

        each(last)
        pltpu.make_async_copy(acc, grad_in, out_sem.at[1]).start()

    def column_sums(ref, k):
        parts = []
        for p in range(2):
            parts.append(
                lax.fori_loop(
                    0, half // 128,
                    lambda i, t: t + jnp.sum(ref[pl.ds(pl.multiple_of(p * half + i * 128, 128), 128), k].astype(f32), axis=0, keepdims=True),
                    jnp.zeros((1, width), f32),
                )
            )
        return parts[0] + parts[1]

    def small_fill():
        n_up = hidden // width
        for i in range(n_up):
            sm_send[0, i : i + 1] = column_sums(dup2, slice(i * width, (i + 1) * width))
        sm_send[0, n_up : n_up + 1] = column_sums(g2, slice(0, width))
        bias = dot_nt(jnp.ones((8, 2 * half), bf16), dqkv_t[...])
        sm_send[0, 3:4] = bias[0:1, :width]
        sm_send[0, 4:5, 0 : bias.shape[1] - width] = bias[0:1, width:]

    def small(i):
        device = (sib, yp, zp, zm, xp)[i]
        return pltpu.make_async_remote_copy(
            src_ref=sm_send.at[i], dst_ref=sm_recv.at[i], send_sem=sm_ss.at[i], recv_sem=sm_rs.at[i],
            device_id=device, device_id_type=MESH,
        )


    sums[...] = jnp.zeros_like(sums)
    sm_send[0] = jnp.zeros_like(sums)
    turn_weights()
    loads[0].wait()
    loads[1].wait()
    for i in range(n_rb):
        make_hidden(rows_of(x, i))
    ff_near()
    for i in range(n_rb):
        ff_far(i)
        if i == n_rb - 2:
            r_copy(n_rb - 1, 1 - x).wait_send()
            for k in range(n_g):
                g_copy(k).start()
    loads[2].wait()
    ff_wave(0)

    def tick(t, _):
        for s in range(6, 0, -1):
            stage(s, t)

        @pl.when(t == n_g - 1)
        def _():
            d_up_far()

        @pl.when(t + 1 < n_ff)
        def _():
            ff_wave(t + 1)

        done = sum(jnp.where(t > k, 1, 0) for k in HEAD_TICKS)
        todo = sum(jnp.where(t >= k, 1, 0) for k in HEAD_TICKS)

        def one(i, _):
            head(i)
            return 0

        lax.fori_loop(done, todo, one, 0)
        at = lambda k: pl.when(t == LATE + k)

        @at(0)
        def _():
            pl.semaphore_signal(free_sem, inc=1, device_id=xp, device_id_type=MESH)
            p_ff(n_ff - 2).wait_send()
            p_ff(n_ff - 1).wait_send()
            branch_far()
            back_far()

        @at(1)
        def _():
            back(x, acc)
            small_fill()
            sm_send[0, 5:7] = sums[0:2]
            small(0).start()

        @at(2)
        def _():
            branch_near()

        for k in range(1, 6):

            @at(1 + k)
            def _():
                small(k - 1).wait_recv()
                total = sm_send[k - 1] + sm_recv[k - 1]
                if k < 4:
                    sm_send[k] = total
                    small(k).start()
                elif k == 4:
                    small_out[...] = total
                    sm_send[4] = total
                    small(4).start()
                else:
                    small_out[5:7] = total[5:7]

        @at(5)
        def _():
            finish()

        return 0

    lax.fori_loop(0, waves + 5, tick, 0)

    def drain(w, _):
        cp("A1", w).wait_send()
        cp("A5", w).wait_send()
        cp("G", w).wait()
        local(w).wait()

        @pl.when(outer)
        def _():
            cp("B1", w).wait_send()
            cp("A2", w).wait_send()

        @pl.when(inner)
        def _():
            for k in ("B2", "A3", "B3", "A4", "B4", "B5a", "B5b"):
                cp(k, w).wait_send()

        return 0

    lax.fori_loop(0, waves, drain, 0)
    for i in range(NP):
        p_at(n_at - NP + i).wait_send()
    for i in range(n_rb):
        xcopy(0, i).wait_send()
        xcopy(1, i).wait_send()
    for i in range(n_rb - 1):
        r_copy(i, x).wait_send()
    for i in range(n_g):
        g_copy(i).wait_send()
    for i in range(5):
        small(i).wait_send()
    out_copy().wait()
    pltpu.make_async_copy(acc, grad_in, out_sem.at[1]).wait()


def mega(g_n, r_n, w_qkv, wo, w_up, w_down, *small):
    half, width = g_n.shape
    rows = 2 * half
    hidden = w_down.shape[0]
    heads = wo.shape[0] // HD
    n_g = width // RW
    waves = 2 * n_g + heads // 2
    n_rb = half // 256
    vm = pl.BlockSpec(memory_space=pltpu.VMEM)
    hbm = pl.BlockSpec(memory_space=pl.ANY)
    dma = pltpu.SemaphoreType.DMA
    v16 = lambda *s: pltpu.VMEM(s, bf16)
    v32 = lambda *s: pltpu.VMEM(s, f32)
    return pl.pallas_call(
        functools.partial(mega_kernel, heads),
        in_specs=[hbm] * 6 + [vm] * len(small),
        out_specs=[hbm, hbm, hbm, vm],
        out_shape=[
            jax.ShapeDtypeStruct((waves, 2 * RW, width), bf16),
            jax.ShapeDtypeStruct((half, width), bf16),
            jax.ShapeDtypeStruct((half, width), f32),
            jax.ShapeDtypeStruct((8, width), f32),
        ],
        scratch_shapes=[
            v16(rows, hidden), v16(rows, hidden), v16(rows, width), v16(rows, width), v16(rows, width),
            v16(heads * 3 * HD, width), v16(heads * HD, width),
            v16(waves, RW, width), v16(2, 2, RW, width), v16(NP, 2, RW, width), v16(waves, RW, width),
            v16(NS, RQ, width), v16(NS, RQ, width), v16(NS, RQ, width), v16(NS, 2 * RQ, width), v16(NS, RQ, width), v16(NS, RQ, width),
            v32(6 * HD, rows), v16(2 * HD, rows), v16(heads * 3 * HD, rows), v16(heads * HD, rows), v16(RW, rows),
            v32(heads * 3 * HD, 128), v32(half, width), v32(256, width),
            v16(2, WC, width), v16(2, width, WC),
            v32(5, 8, width), v32(5, 8, width), v32(8, width),
            dma((len(KINDS), waves)), dma((len(KINDS), waves)), dma((waves,)), dma((N_LOADS,)), dma((n_rb,)), dma((n_rb,)),
            dma((n_g,)), dma((n_g,)), dma((2, n_rb)), dma((2, n_rb)), dma((2,)), dma((2,)), dma((5,)), dma((5,)), dma((2,)), pltpu.SemaphoreType.REGULAR,
        ],
        compiler_params=pltpu.CompilerParams(collective_id=0, has_side_effects=True, vmem_limit_bytes=63 * 2**20),
        name="attention_and_sums",
    )(g_n, r_n, w_qkv, wo, w_up, w_down, *small)


def widen_kernel(n_g, src, down, up, qkv, out):
    i = pl.program_id(0)
    width = src.shape[2]
    side = lambda k: lax.broadcasted_iota(jnp.int32, (RW, RW), k)
    eye = jnp.where(side(0) == side(1), 1.0, 0.0).astype(bf16)

    @pl.when(i < n_g)
    def _():
        for c in range(2):
            for k in range(width // RW):
                down[c * width + k * RW : c * width + (k + 1) * RW] = dot_nt(
                    eye, src[0, c * RW : (c + 1) * RW, k * RW : (k + 1) * RW]
                )

    @pl.when(jnp.logical_and(i >= n_g, i < 2 * n_g))
    def _():
        for c in range(2):
            up[:, c * width : (c + 1) * width] = src[0, c * RW : (c + 1) * RW].astype(f32)

    @pl.when(i >= 2 * n_g)
    def _():
        hq = 3 * HD
        for k in range(width // RW):
            cols = slice(k * RW, (k + 1) * RW)
            both = jnp.concatenate([src[0, 0:hq, cols], src[0, RW : RW + hq, cols]], axis=0)
            qkv[cols] = dot_nt(eye, both)
        for c in range(2):
            out[c * HD : (c + 1) * HD] = src[0, c * RW + hq : (c + 1) * RW].astype(f32)


def widen(red, hidden):
    waves, _, width = red.shape
    n_g = width // RW
    n_at = waves - 2 * n_g
    clip = lambda i, first, n: jnp.minimum(jnp.maximum(i - first, 0), n - 1)
    return pl.pallas_call(
        functools.partial(widen_kernel, n_g),
        grid=(waves,),
        in_specs=[pl.BlockSpec((1, 2 * RW, width), lambda i: (i, 0, 0))],
        out_specs=[
            pl.BlockSpec((hidden, RW), lambda i: (0, clip(i, 0, n_g))),
            pl.BlockSpec((RW, hidden), lambda i: (clip(i, n_g, n_g), 0)),
            pl.BlockSpec((width, 6 * HD), lambda i: (0, clip(i, 2 * n_g, n_at))),
            pl.BlockSpec((2 * HD, width), lambda i: (clip(i, 2 * n_g, n_at), 0)),
        ],
        out_shape=[
            jax.ShapeDtypeStruct((hidden, width), f32),
            jax.ShapeDtypeStruct((width, hidden), f32),
            jax.ShapeDtypeStruct((width, n_at * 6 * HD), f32),
            jax.ShapeDtypeStruct((n_at * 2 * HD, width), f32),
        ],
        compiler_params=pltpu.CompilerParams(vmem_limit_bytes=48 * 2**20),
        name="widen",
    )(red)


def shards(residual, ln_gain, ln_bias, w_qkv, b_qkv, w_out, b_out, w_up, b_up, w_down, b_down, grad_out):
    width = residual.shape[1]
    cosine, sine = turn_tables(2 * residual.shape[0])
    cs = jnp.concatenate([cosine.T, sine.T])
    rows = [v[None] for v in (b_qkv, b_up)] + [cs] + [v[None] for v in (ln_gain, ln_bias, b_out, b_down)]
    red, out, grad_in, small = mega(grad_out, residual, w_qkv, w_out, w_up, w_down, *rows)
    grad_w_down, grad_w_up, grad_w_qkv, grad_w_out = widen(red, w_down.shape[0])
    gb_up = small[: b_up.shape[0] // width].reshape(-1)
    gb_out = small[2]
    gb_qkv = small[3:5].reshape(-1)[: b_qkv.shape[0]]
    return out, grad_in, small[5], small[6], grad_w_qkv, gb_qkv, grad_w_out, gb_out, grad_w_up, gb_up, grad_w_down, gb_out


def contract_rows(left, right):
    return lax.dot_general(
        left, right, (((0,), (0,)), ((), ())), preferred_element_type=jnp.float32
    )


def contract_cols(left, right):
    return lax.dot_general(
        left, right, (((1,), (1,)), ((), ())), preferred_element_type=jnp.float32
    )


def turn_heads(heads, cosine, sine):
    half_rot = ROT // 2
    first = heads[:, :, :half_rot]
    second = heads[:, :, half_rot:ROT]
    rest = heads[:, :, ROT:]
    cos_rows = cosine[:, None, :]
    sin_rows = sine[:, None, :]
    return jnp.concatenate(
        [first * cos_rows - second * sin_rows, second * cos_rows + first * sin_rows, rest], axis=2
    )


def undo_turn(heads, cosine, sine):
    half_rot = ROT // 2
    first = heads[:, :, :half_rot]
    second = heads[:, :, half_rot:ROT]
    rest = heads[:, :, ROT:]
    cos_rows = cosine[:, None, :]
    sin_rows = sine[:, None, :]
    return jnp.concatenate(
        [first * cos_rows + second * sin_rows, second * cos_rows - first * sin_rows, rest], axis=2
    )


def shards_any(
    residual, ln_gain, ln_bias, w_qkv, b_qkv, w_out, b_out, w_up, b_up, w_down, b_down, grad_out
):
    rows_here = residual.shape[0]
    head_cols = w_out.shape[0]
    heads_here = head_cols // HD
    resid_wide = residual.astype(jnp.float32)
    average = jnp.mean(resid_wide, axis=1, keepdims=True)
    centered = resid_wide - average
    variance = jnp.mean(centered * centered, axis=1, keepdims=True)
    inv_std = lax.rsqrt(variance + epsilon)
    normed = centered * inv_std
    h_local = (normed * ln_gain + ln_bias).astype(jnp.bfloat16)
    h_full = lax.all_gather(h_local, "tensor", axis=0, tiled=True)
    group_rows = h_full.shape[0]
    seqlen = min(LEN_MAX, group_rows)
    seq_count = group_rows // seqlen
    qkv = jnp.dot(h_full, w_qkv, preferred_element_type=jnp.float32) + b_qkv
    up_lin = jnp.dot(h_full, w_up, preferred_element_type=jnp.float32) + b_up
    act_wide, gelu_back = jax.vjp(functools.partial(jax.nn.gelu, approximate=False), up_lin)
    act = act_wide.astype(jnp.bfloat16)
    cosine, sine = turn_tables(seqlen)
    causal = jnp.arange(seqlen)[:, None] >= jnp.arange(seqlen)[None, :]
    scale = 1.0 / math.sqrt(HD)

    def attend(block):
        queries = turn_heads(block[:, :, 0, :], cosine, sine).astype(jnp.bfloat16)
        key_rows = turn_heads(block[:, :, 1, :], cosine, sine).astype(jnp.bfloat16)
        value_rows = block[:, :, 2, :].astype(jnp.bfloat16)
        scores = (
            jnp.einsum("qhd,khd->hqk", queries, key_rows, preferred_element_type=jnp.float32)
            * scale
        )
        scores = jnp.where(causal[None], scores, -1e30)
        peak = jnp.max(scores, axis=2, keepdims=True)
        raised = jnp.exp(scores - peak)
        totals = jnp.sum(raised, axis=2, keepdims=True)
        probs = raised / totals
        attended = jnp.einsum(
            "hqk,khd->qhd",
            probs.astype(jnp.bfloat16),
            value_rows,
            preferred_element_type=jnp.float32,
        ).astype(jnp.bfloat16)
        log_total = peak[:, :, 0] + jnp.log(totals[:, :, 0])
        return (queries, key_rows, value_rows, attended, log_total)

    blocks = qkv.reshape(seq_count, seqlen, heads_here, 3, HD)
    queries, key_rows, value_rows, attended, log_total = lax.map(attend, blocks)
    attn_rows = attended.reshape(group_rows, head_cols)
    act_part = lax.slice_in_dim(act, 0, lax.axis_size("tensor") * rows_here, axis=0)
    branch = lax.psum_scatter(
        jnp.dot(attn_rows, w_out, preferred_element_type=jnp.float32)
        + jnp.dot(act_part, w_down, preferred_element_type=jnp.float32),
        "tensor",
        scatter_dimension=0,
        tiled=True,
    )
    out = (resid_wide + branch + b_out + b_down).astype(jnp.bfloat16)
    grad_local = grad_out.astype(jnp.float32)
    grad_full = lax.all_gather(grad_out, "tensor", axis=0, tiled=True)
    grad_w_out = contract_rows(attn_rows, grad_full)
    grad_w_down = contract_rows(act, grad_full)
    d_attended = contract_cols(grad_full, w_out).astype(jnp.bfloat16)
    d_act = contract_cols(grad_full, w_down)
    d_up = gelu_back(d_act)[0].astype(jnp.bfloat16)
    grad_b_up = jnp.sum(d_up, axis=0, dtype=jnp.float32)

    def attend_back(items):
        query_part, key_part, value_part, log_part, d_part = items
        scores = (
            jnp.einsum("qhd,khd->hqk", query_part, key_part, preferred_element_type=jnp.float32)
            * scale
        )
        probs = jnp.where(causal[None], jnp.exp(scores - log_part[:, :, None]), 0.0)
        grad_values = jnp.einsum(
            "hqk,qhd->khd", probs.astype(jnp.bfloat16), d_part, preferred_element_type=jnp.float32
        )
        d_probs = jnp.einsum("qhd,khd->hqk", d_part, value_part, preferred_element_type=jnp.float32)
        d_scores = (probs * (d_probs - jnp.sum(d_probs * probs, axis=2, keepdims=True))).astype(
            jnp.bfloat16
        )
        d_query = (
            jnp.einsum("hqk,khd->qhd", d_scores, key_part, preferred_element_type=jnp.float32)
            * scale
        )
        d_key = (
            jnp.einsum("hqk,qhd->khd", d_scores, query_part, preferred_element_type=jnp.float32)
            * scale
        )
        return jnp.stack(
            [undo_turn(d_query, cosine, sine), undo_turn(d_key, cosine, sine), grad_values], axis=2
        )

    d_blocks = d_attended.reshape(seq_count, seqlen, heads_here, HD)
    d_qkv = lax.map(attend_back, (queries, key_rows, value_rows, log_total, d_blocks))
    d_qkv = d_qkv.reshape(group_rows, 3 * head_cols).astype(jnp.bfloat16)
    grad_b_qkv = jnp.sum(d_qkv, axis=0, dtype=jnp.float32)
    grad_w_qkv = contract_rows(h_full, d_qkv)
    grad_w_up = contract_rows(h_full, d_up)
    d_hidden = lax.psum_scatter(
        contract_cols(d_qkv, w_qkv) + contract_cols(d_up, w_up),
        "tensor",
        scatter_dimension=0,
        tiled=True,
    )
    gain_local = jnp.sum(d_hidden * normed, axis=0)
    bias_local = jnp.sum(d_hidden, axis=0)
    d_hat = d_hidden * ln_gain
    grad_in = grad_local + inv_std * (
        d_hat
        - jnp.mean(d_hat, axis=1, keepdims=True)
        - normed * jnp.mean(d_hat * normed, axis=1, keepdims=True)
    )
    out_bias = jnp.sum(grad_full, axis=0, dtype=jnp.float32)
    grad_w_qkv, grad_b_qkv, grad_w_out, grad_w_up, grad_b_up, grad_w_down, grad_b_out = lax.psum(
        (grad_w_qkv, grad_b_qkv, grad_w_out, grad_w_up, grad_b_up, grad_w_down, out_bias), "dp"
    )
    grad_ln_gain, grad_ln_bias = lax.psum((gain_local, bias_local), ("dp", "tensor"))
    return (
        out,
        grad_in,
        grad_ln_gain,
        grad_ln_bias,
        grad_w_qkv,
        grad_b_qkv,
        grad_w_out,
        grad_b_out,
        grad_w_up,
        grad_b_up,
        grad_w_down,
        grad_b_out,
    )


def solution(mesh):
    small_slice = mesh.shape["dp"] == 16 and mesh.shape["tensor"] == 2
    return jax.shard_map(
        shards if small_slice else shards_any,
        mesh=mesh,
        in_specs=(
            P(("dp", "tensor"), None),
            P(),
            P(),
            P(None, "tensor"),
            P("tensor"),
            P("tensor", None),
            P(),
            P(None, "tensor"),
            P("tensor"),
            P("tensor", None),
            P(),
            P(("dp", "tensor"), None),
        ),
        out_specs=(
            P(("dp", "tensor"), None),
            P(("dp", "tensor"), None),
            P(),
            P(),
            P(None, "tensor"),
            P("tensor"),
            P("tensor", None),
            P(),
            P(None, "tensor"),
            P("tensor"),
            P("tensor", None),
            P(),
        ),
        check_vma=False,
    )
```

```python
import functools
import math

import jax
import jax.numpy as jnp
import numpy as np
from jax import lax
from jax.experimental import pallas as pl
from jax.experimental.pallas import tpu as pltpu
from jax.sharding import PartitionSpec as P

HD = 64
ROT = 16
LEN_MAX = 1024
epsilon = 1e-05
MESH = pl.DeviceIdType.MESH
f32 = jnp.float32
bf16 = jnp.bfloat16


def dot(left, right):
    return lax.dot_general(left, right, (((1,), (0,)), ((), ())), preferred_element_type=f32)


def dot_nt(left, right):
    return lax.dot_general(left, right, (((1,), (1,)), ((), ())), preferred_element_type=f32)


def turn_tables(seqlen):
    half_rot = ROT // 2
    exponent = jnp.arange(half_rot, dtype=f32) * (2.0 / ROT)
    inverse = 1.0 / 10000.0**exponent
    places = jnp.arange(seqlen, dtype=f32)
    angles = places[:, None] * inverse[None, :]
    return (jnp.cos(angles), jnp.sin(angles))


def turn(t, cos, sin, sign):
    a, b = t[0:8], t[8:16]
    return jnp.concatenate([a * cos - sign * (b * sin), b * cos + sign * (a * sin), t[16:]], axis=0)


def attend_head(q_t, k_t, v_t, do_t, cos, sin, blk=256):
    seq = q_t.shape[1]
    nb = seq // blk
    qs = turn(q_t, cos, sin, 1.0).astype(bf16) * jnp.asarray(0.125, bf16)
    kb = turn(k_t, cos, sin, 1.0).astype(bf16)
    vb = v_t.astype(bf16)
    keys, values, queries, grads = kb.T, vb.T, qs.T, do_t.T
    seen = lax.broadcasted_iota(jnp.int32, (blk, blk), 0) <= lax.broadcasted_iota(jnp.int32, (blk, blk), 1)
    outs, dqs, dv_sum, dk_sum = [], [], [None] * nb, [None] * nb

    def products(i):
        kk, sl = (i + 1) * blk, slice(i * blk, (i + 1) * blk)
        return dot(keys[:kk], qs[:, sl]), dot(values[:kk], do_t[:, sl])

    def gather(sums, i, v):
        for j in range(i + 1):
            a = v[j * blk : (j + 1) * blk]
            sums[j] = a if sums[j] is None else sums[j] + a

    def back(i, p, dp):
        kk, sl = (i + 1) * blk, slice(i * blk, (i + 1) * blk)
        ds = (p * (dp - jnp.sum(p * dp, axis=0, keepdims=True))).astype(bf16)
        dqs.append(dot(kb[:, :kk], ds) * 0.125)
        gather(dk_sum, i, dot(ds, queries[sl]))

    ahead, behind = products(0), None
    for i in range(nb):
        kk, sl = (i + 1) * blk, slice(i * blk, (i + 1) * blk)
        s, dp = ahead
        if i + 1 < nb:
            ahead = products(i + 1)
        diag = jnp.where(seen, s[i * blk :], -1e30)
        s = jnp.concatenate([s[: i * blk], diag], axis=0) if i else diag
        p = jnp.exp(s - jnp.max(s, axis=0, keepdims=True))
        p = p * (1.0 / jnp.sum(p, axis=0, keepdims=True))
        pb = p.astype(bf16)
        outs.append(dot(vb[:, :kk], pb).astype(bf16))
        gather(dv_sum, i, dot(pb, grads[sl]))
        if behind is not None:
            back(*behind)
        behind = (i, p, dp)
    back(*behind)
    dq_t = turn(jnp.concatenate(dqs, axis=1), cos, sin, -1.0)
    dk_t = turn(jnp.concatenate(dk_sum, axis=0).T, cos, sin, -1.0)
    dv_t = jnp.concatenate(dv_sum, axis=0).T
    return jnp.concatenate(outs, axis=1), dq_t, dk_t, dv_t


def gelu_and_slope(u):
    half = 0.5 + 0.5 * lax.erf(u * (1.0 / math.sqrt(2.0)))
    bell = jnp.exp(u * u * -0.5) * (1.0 / math.sqrt(2.0 * math.pi))
    return u * half, half + u * bell


RW = 256
RQ = RW // 4
NS = 4
NP = 2
KINDS = ("P", "A1", "A2", "A3", "A4", "A5", "B1", "B2", "B3", "B4", "B5a", "B5b", "G")
KI = {k: i for i, k in enumerate(KINDS)}
TURNS = ((6, 5, 4), (3, 2, 1), ())
FF_AT = (1, 4, 7, 22, 24, 27, 30)
HEAD_AT = (8, 9, 10, 12, 13, 15, 16, 18)
PLAN = {
    "branch_ff": 0, "free": 12, "d_up": 19, "branch_far": 21, "back_far": 25, "back_near": 28, "small": 31,
    "branch_near": 36, "finish": 45,
}
SMALL_AT = (34, 37, 40, 43, 46)
BC = 512
WC = 256
N_LOADS = 6


def mega_kernel(
    heads,
    g_n, r_n, w_qkv, wo, w_up, w_down, bq, bu, cs, ln_gain, ln_bias, b_out, b_down,
    red, out, grad_in, small_out,
    act2, dup2, h2, g2, r2, w_t2, wo2, w_up2, w_dn2, x_buf, fw, ag, ra1, ra2, ra3, rb1, rb2, rb3,
    qkv_s, do_s, dqkv_t, att_t, t_buf, tq, acc,
    sm_send, sm_recv, sums,
    ss, rs, loc_sem, load_sem, r_ss, r_rs, g_ss, g_rs, x_ss, x_rs, sm_ss, sm_rs, out_sem, free_sem, y_free, z_free, m_free,
):
    half, width = g_n.shape
    hidden = w_down.shape[0]
    n_g = width // RW
    n_at = heads // 2
    n_ff = 2 * n_g
    waves = n_ff + n_at
    first_up = n_g + n_at
    dp, x = lax.axis_index("dp"), lax.axis_index("tensor")
    c, y, z = lax.rem(dp, 2), lax.rem(dp // 2, 2), dp // 4
    dev = lambda zz, yy, cc, xx: (zz * 4 + yy * 2 + cc, xx)
    sib = dev(z, y, 1 - c, x)
    yp = dev(z, 1 - y, c, x)
    zp = dev(z + 1 - 2 * lax.rem(z, 2), y, c, x)
    zm = dev(3 - z, y, c, x)
    xp = dev(z, y, c, 1 - x)
    inner = jnp.logical_or(z == 1, z == 2)
    outer = jnp.logical_not(inner)
    near = pl.ds(pl.multiple_of(x * half, half), half)
    far = pl.ds(pl.multiple_of((1 - x) * half, half), half)

    loads = []
    staged = act2.at[:, pl.ds(0, w_qkv.shape[1])]
    for src, dst in (
        (w_qkv, staged), (r_n, r2.at[near]), (w_up, w_up2), (g_n, g2.at[near]), (w_down, w_dn2), (wo, wo2),
    ):
        loads.append(pltpu.make_async_copy(src, dst, load_sem.at[len(loads)]))
    for k in loads:
        k.start()

    barrier = pltpu.get_barrier_semaphore()
    for d in (xp, sib, yp, zp, zm):
        pl.semaphore_signal(barrier, inc=1, device_id=d, device_id_type=MESH)
    pl.semaphore_wait(barrier, 5)

    def g_copy(i):
        cols = pl.ds(pl.multiple_of(i * RW, RW), RW)
        return pltpu.make_async_remote_copy(
            src_ref=g_n.at[:, cols], dst_ref=g2.at[near, cols], send_sem=g_ss.at[i], recv_sem=g_rs.at[i],
            device_id=xp, device_id_type=MESH,
        )

    def g_arrives(i):
        cols = pl.ds(pl.multiple_of(i * RW, RW), RW)
        pltpu.make_async_remote_copy(
            src_ref=g_n.at[:, cols], dst_ref=g2.at[far, cols], send_sem=g_ss.at[i], recv_sem=g_rs.at[i],
            device_id=xp, device_id_type=MESH,
        ).wait_recv()

    rb = 256
    n_rb = half // rb

    def rows_of(who, i):
        return pl.ds(pl.multiple_of(who * half + i * rb, rb), rb)

    def r_copy(i, who):
        return pltpu.make_async_remote_copy(
            src_ref=r_n.at[pl.ds(pl.multiple_of(i * rb, rb), rb)], dst_ref=r2.at[rows_of(who, i)],
            send_sem=r_ss.at[i], recv_sem=r_rs.at[i], device_id=xp, device_id_type=MESH,
        )

    for i in range(n_rb):
        r_copy(i, x).start()


    a_mine = pl.ds(pl.multiple_of(y * RQ, RQ), RQ)
    a_other = pl.ds(pl.multiple_of((1 - y) * RQ, RQ), RQ)
    zi = jnp.where(z == 2, 1, 0)
    b_mine = pl.ds(pl.multiple_of(2 * RQ + zi * RQ, RQ), RQ)
    b_other = pl.ds(pl.multiple_of(2 * RQ + (1 - zi) * RQ, RQ), RQ)
    b_all = pl.ds(2 * RQ, 2 * RQ)

    def rc(kind, w, src, dst, device):
        k = KI[kind]
        return pltpu.make_async_remote_copy(
            src_ref=src, dst_ref=dst, send_sem=ss.at[k, w], recv_sem=rs.at[k, w], device_id=device, device_id_type=MESH
        )

    def cp(kind, w):
        s = lax.rem(w, NS)
        if kind == "A1":
            return rc(kind, w, x_buf.at[w, a_other], ra1.at[s], yp)
        if kind == "A2":
            return rc(kind, w, x_buf.at[w, a_mine], ra2.at[s], zp)
        if kind == "A3":
            return rc(kind, w, x_buf.at[w, a_mine], ra3.at[s], zm)
        if kind == "A4":
            return rc(kind, w, x_buf.at[w, a_mine], x_buf.at[w, a_mine], zp)
        if kind == "A5":
            return rc(kind, w, x_buf.at[w, a_mine], x_buf.at[w, a_mine], yp)
        if kind == "B1":
            return rc(kind, w, x_buf.at[w, b_all], rb1.at[s], zp)
        if kind == "B2":
            return rc(kind, w, x_buf.at[w, b_other], rb2.at[s], zm)
        if kind == "B3":
            return rc(kind, w, x_buf.at[w, b_mine], rb3.at[s], yp)
        if kind == "B4":
            return rc(kind, w, x_buf.at[w, b_mine], x_buf.at[w, b_mine], zm)
        if kind == "B5a":
            return rc(kind, w, x_buf.at[w, b_mine], x_buf.at[w, b_mine], zp)
        if kind == "B5b":
            return rc(kind, w, x_buf.at[w, b_other], x_buf.at[w, b_other], zp)
        if kind == "G":
            there = red.at[w, pl.ds(pl.multiple_of(c * RW, RW), RW)]
            return rc(kind, w, x_buf.at[w], there, sib)

    def wave_of(k):
        return jnp.where(k < n_g, k, k + n_at)

    def p_ff(k):
        return rc("P", wave_of(k), fw.at[lax.rem(k, 2), 1 - c], x_buf.at[wave_of(k)], sib)

    def p_at(j):
        return rc("P", n_g + j, ag.at[lax.rem(j, NP), 1 - c], x_buf.at[n_g + j], sib)

    def local(w):
        here = red.at[w, pl.ds(pl.multiple_of(c * RW, RW), RW)]
        return pltpu.make_async_copy(x_buf.at[w], here, loc_sem.at[w])

    def add(a, b):
        return (a.astype(f32) + b.astype(f32)).astype(bf16)

    def give(sem, device):
        pl.semaphore_signal(sem, inc=1, device_id=device, device_id_type=MESH)

    def stage(s, t):
        w = t - (s - 1)
        ok = jnp.logical_and(w >= 0, w < waves)
        slot = lax.rem(w, NS)
        if s == 1:

            of_heads = jnp.logical_and(w >= n_g, w < first_up)

            @pl.when(jnp.logical_and(ok, jnp.logical_not(of_heads)))
            def _():
                k = jnp.where(w < n_g, w, w - n_at)
                p_ff(k).wait_recv()
                x_buf[w] = add(x_buf[w], fw[lax.rem(k, 2), c])

            @pl.when(jnp.logical_and(ok, of_heads))
            def _():
                p_at(w - n_g).wait_recv()
                x_buf[w] = add(x_buf[w], ag[lax.rem(w - n_g, NP), c])

            @pl.when(ok)
            def _():
                cp("A1", w).start()

                @pl.when(outer)
                def _():
                    cp("B1", w).start()

        if s == 2:

            @pl.when(ok)
            def _():
                cp("A1", w).wait()
                give(y_free, yp)
                x_buf[w, a_mine] = add(x_buf[w, a_mine], ra1[slot])

                @pl.when(outer)
                def _():
                    cp("A2", w).start()

                @pl.when(inner)
                def _():
                    cp("B1", w).wait_recv()
                    x_buf[w, b_all] = add(x_buf[w, b_all], rb1[slot])
                    cp("B2", w).start()

        if s == 3:

            @pl.when(jnp.logical_and(ok, outer))
            def _():
                cp("B1", w).wait_send()
                cp("A2", w).wait_send()
                give(z_free, zp)

            @pl.when(jnp.logical_and(ok, inner))
            def _():
                cp("A2", w).wait_recv()
                x_buf[w, a_mine] = add(x_buf[w, a_mine], ra2[slot])
                cp("A3", w).start()
                cp("B2", w).wait()
                give(m_free, zm)
                x_buf[w, b_mine] = add(x_buf[w, b_mine], rb2[slot])
                cp("B3", w).start()

        if s == 4:

            @pl.when(jnp.logical_and(ok, inner))
            def _():
                cp("A3", w).wait()
                x_buf[w, a_mine] = add(x_buf[w, a_mine], ra3[slot])
                pl.semaphore_wait(z_free, 1)
                cp("A4", w).start()
                pl.semaphore_wait(y_free, 1)
                cp("A5", w).start()
                cp("B3", w).wait()
                x_buf[w, b_mine] = add(x_buf[w, b_mine], rb3[slot])
                pl.semaphore_wait(m_free, 1)
                cp("B4", w).start()
                cp("B5a", w).start()

        if s == 5:

            @pl.when(jnp.logical_and(ok, inner))
            def _():
                cp("B4", w).wait_recv()
                cp("B5b", w).start()

            @pl.when(jnp.logical_and(ok, outer))
            def _():
                cp("A4", w).wait_recv()
                pl.semaphore_wait(y_free, 1)
                cp("A5", w).start()

        if s == 6:

            @pl.when(ok)
            def _():
                cp("A5", w).wait_recv()

                @pl.when(outer)
                def _():
                    cp("B5a", w).wait_recv()
                    cp("B5b", w).wait_recv()

                cp("G", w).start()
                local(w).start()


    def ff_wave(k):
        @pl.when(k >= 2)
        def _():
            p_ff(k - 2).wait_send()

        def product(src, full):
            t_buf[...] = src.T

            def block(n, _):
                cols = pl.ds(pl.multiple_of(n * BC, BC), BC)
                per = width // BC
                fw[lax.rem(k, 2), n // per, :, pl.ds(pl.multiple_of(lax.rem(n, per) * BC, BC), BC)] = dot(
                    t_buf[...], full[:, cols]
                ).astype(bf16)
                return 0

            lax.fori_loop(0, hidden // BC, block, 0)

        @pl.when(k < n_g)
        def _():
            g_arrives(k)
            product(g2[:, pl.ds(pl.multiple_of(k * RW, RW), RW)], act2)

        @pl.when(k >= n_g)
        def _():
            product(h2[:, pl.ds(pl.multiple_of((k - n_g) * RW, RW), RW)], dup2)

        p_ff(k).start()

    n_hid = hidden // WC

    def norm(rows):
        r = r2[rows].astype(f32)
        centered = r - jnp.mean(r, axis=1, keepdims=True)
        inv = lax.rsqrt(jnp.mean(centered * centered, axis=1, keepdims=True) + epsilon)
        return r, centered * inv, inv

    def make_hidden(rows):
        h2[rows] = (norm(rows)[1] * ln_gain[...][None] + ln_bias[...][None]).astype(bf16)

    def turn_weights():
        def body(n, _):
            here = pl.ds(pl.multiple_of(n * WC, WC), WC)
            w_t2[here] = act2[:, here].T
            return 0

        lax.fori_loop(0, w_qkv.shape[1] // WC, body, 0)

    def over(total, size, body):
        def step(n, _):
            body(pl.ds(pl.multiple_of(n * size, size), size))
            return 0

        lax.fori_loop(0, total // size, step, 0)

    def ff_near():
        def body(cols):
            a, slope = gelu_and_slope(dot(h2[near], w_up2[:, cols]) + bu[cols][None])
            act2[near, cols] = a.astype(bf16)
            dup2[near, cols] = (dot_nt(g2[near], w_dn2[cols]) * slope).astype(bf16)

        over(hidden, WC, body)

    def ff_far(i):
        r = rows_of(1 - x, i)
        r_copy(i, 1 - x).wait_recv()
        make_hidden(r)

        def body(cols):
            a, slope = gelu_and_slope(dot(h2[r], w_up2[:, cols]) + bu[cols][None])
            act2[r, cols] = a.astype(bf16)
            dup2[r, cols] = slope.astype(bf16)

        over(hidden, BC, body)

    def d_up_far():
        def body(cols):
            dup2[far, cols] = (dot_nt(g2[far], w_dn2[cols]) * dup2[far, cols].astype(f32)).astype(bf16)

        over(hidden, WC, body)


    cos, sin = cs[0:8], cs[8:16]
    hq, hv = 3 * HD, HD

    def head(t):
        odd = lax.rem(t, 2)
        j = t // 2
        pair_q = pl.ds(pl.multiple_of(j * 2 * hq, 2 * HD), 2 * hq)
        pair_v = pl.ds(pl.multiple_of(j * 2 * hv, 2 * HD), 2 * hv)

        @pl.when(odd == 0)
        def _():
            bias = jnp.broadcast_to(bq[pl.ds(pl.multiple_of(j * 2 * hq, 128), 2 * hq)][None], (128, 2 * hq)).T
            qkv_s[...] = dot_nt(w_t2[pair_q], h2[...]) + bias[:, 0:1]
            do_s[...] = dot_nt(wo2[pair_v], g2[...]).astype(bf16)

        part = lambda i: qkv_s[pl.ds(pl.multiple_of(odd * hq + i * HD, HD), HD)]
        o, dq, dk, dv = attend_head(
            part(0), part(1), part(2), do_s[pl.ds(pl.multiple_of(odd * hv, HD), HD)], cos, sin
        )
        att_t[pl.ds(pl.multiple_of(t * hv, HD), HD)] = o
        for i, v in enumerate((dq, dk, dv)):
            dqkv_t[pl.ds(pl.multiple_of(t * hq + i * HD, HD), HD)] = v.astype(bf16)

        @pl.when(odd == 1)
        def _():
            slot = lax.rem(j, NP)

            @pl.when(j >= NP)
            def _():
                p_at(j - NP).wait_send()

            gq = dot(dqkv_t[pair_q], h2[...]).astype(bf16)
            gv = dot(att_t[pair_v], g2[...]).astype(bf16)
            for i in range(2):
                ag[slot, i, 0:hq] = gq[i * hq : (i + 1) * hq]
                ag[slot, i, hq : hq + hv] = gv[i * hv : (i + 1) * hv]
            p_at(j).start()


    def xcopy(which, i):
        there = act2.at[rows_of(x, i), pl.ds(which * width, width)]
        return pltpu.make_async_remote_copy(
            src_ref=ag.at[which, i], dst_ref=there, send_sem=x_ss.at[which, i], recv_sem=x_rs.at[which, i],
            device_id=xp, device_id_type=MESH,
        )

    def arrived(which, i):
        return act2.at[rows_of(1 - x, i), pl.ds(which * width, width)]

    def each(body):
        def step(i, _):
            body(i, pl.ds(pl.multiple_of(i * rb, rb), rb))
            return 0

        lax.fori_loop(0, n_rb, step, 0)

    def branch_ff_far():
        def body(cols):
            acc[:, cols] = dot(act2[far], w_dn2[:, cols])

        over(width, WC, body)

    def back(who):
        def rows(i, here):
            r = rows_of(who, i)
            tq[...] = dqkv_t[:, r].T
            _, normed, _ = norm(r)

            def body(cols):
                acc[here, cols] = dot(tq[...], w_t2[:, cols]) + dot_nt(dup2[r], w_up2[cols])

            over(width, WC, body)
            d = acc[here]
            sums[0:1] = sums[0:1] + jnp.sum(d * normed, axis=0, keepdims=True)
            sums[1:2] = sums[1:2] + jnp.sum(d, axis=0, keepdims=True)
            if who is not x:
                ag[1, i] = d.astype(bf16)
                xcopy(1, i).start()

        each(rows)

    def out_copy():
        return pltpu.make_async_copy(act2.at[far, pl.ds(0, width)], out, out_sem.at[0])

    def branch_far():
        pl.semaphore_wait(free_sem, 1)

        def send(i, here):
            ag[0, i] = (acc[here] + dot(att_t[:, rows_of(1 - x, i)].T, wo2[...])).astype(bf16)
            xcopy(0, i).start()

        each(send)

    def branch_near():
        for i in range(n_rb):
            r = rows_of(x, i)
            xcopy(0, i).wait_recv()
            at = att_t[:, r].T
            t_buf[:, 0 : at.shape[1]] = at

            def body(cols):
                total = dot(t_buf[:, 0 : at.shape[1]], wo2[:, cols]) + dot(act2[r, :], w_dn2[:, cols])
                total = total + (b_out[cols] + b_down[cols])[None] + r2[r, cols].astype(f32)
                there = act2.at[rows_of(1 - x, i), cols]
                there[...] = (total + there[...].astype(f32)).astype(bf16)

            over(width, WC, body)
        out_copy().start()

    def finish():
        def last(i, here):
            xcopy(1, i).wait_recv()
            _, normed, inv = norm(rows_of(x, i))
            d_hat = (acc[here] + arrived(1, i)[...].astype(f32)) * ln_gain[...][None]
            first = jnp.mean(d_hat, axis=1, keepdims=True)
            second = jnp.mean(d_hat * normed, axis=1, keepdims=True)
            acc[here] = g2[rows_of(x, i)].astype(f32) + inv * (d_hat - first - normed * second)

        each(last)
        pltpu.make_async_copy(acc, grad_in, out_sem.at[1]).start()

    def small_fill():
        n_up = hidden // width
        ones = jnp.ones((8, 2 * half), bf16)
        up = dot(ones, dup2[...])
        for i in range(n_up):
            sm_send[0, i : i + 1] = up[0:1, i * width : (i + 1) * width]
        sm_send[0, n_up : n_up + 1] = dot(ones, g2[...])[0:1]
        bias = dot_nt(ones, dqkv_t[...])
        sm_send[0, 3:4] = bias[0:1, :width]
        sm_send[0, 4:5, 0 : bias.shape[1] - width] = bias[0:1, width:]

    def small(i):
        device = (sib, yp, zp, zm, xp)[i]
        return pltpu.make_async_remote_copy(
            src_ref=sm_send.at[i], dst_ref=sm_recv.at[i], send_sem=sm_ss.at[i], recv_sem=sm_rs.at[i],
            device_id=device, device_id_type=MESH,
        )


    sums[...] = jnp.zeros_like(sums)
    sm_send[0] = jnp.zeros_like(sums)
    loads[0].wait()
    turn_weights()
    loads[1].wait()
    for i in range(n_rb):
        make_hidden(rows_of(x, i))
    for i in range(2, 5):
        loads[i].wait()
    ff_near()
    for i in range(n_rb):
        ff_far(i)
        if i == n_rb - 2:
            r_copy(n_rb - 1, 1 - x).wait_send()
            for k in range(n_g):
                g_copy(k).start()
    loads[5].wait()
    ff_wave(0)

    def turn_of(v, _):
        t = v // len(TURNS)
        for r, stages in enumerate(TURNS):

            @pl.when(lax.rem(v, len(TURNS)) == r)
            def _():
                for k in stages:
                    stage(k, t)

        at = lambda k: pl.when(v == PLAN[k])

        @at("branch_ff")
        def _():
            branch_ff_far()

        @at("free")
        def _():
            pl.semaphore_signal(free_sem, inc=1, device_id=xp, device_id_type=MESH)

        @at("d_up")
        def _():
            d_up_far()

        done = sum(jnp.where(v > k, 1, 0) for k in FF_AT)
        todo = sum(jnp.where(v >= k, 1, 0) for k in FF_AT)

        @pl.when(todo > done)
        def _():
            ff_wave(todo)

        done_h = sum(jnp.where(v > k, 1, 0) for k in HEAD_AT)
        todo_h = sum(jnp.where(v >= k, 1, 0) for k in HEAD_AT)

        @pl.when(todo_h > done_h)
        def _():
            head(done_h)

        @at("branch_far")
        def _():
            for i in range(NP):
                p_at(n_at - NP + i).wait_send()
            branch_far()

        @at("back_far")
        def _():
            back(1 - x)

        @at("back_near")
        def _():
            back(x)

        @at("small")
        def _():
            small_fill()
            sm_send[0, 5:7] = sums[0:2]
            small(0).start()

        for k in range(1, 6):

            @pl.when(v == SMALL_AT[k - 1])
            def _():
                small(k - 1).wait_recv()
                total = sm_send[k - 1] + sm_recv[k - 1]
                if k < 4:
                    sm_send[k] = total
                    small(k).start()
                elif k == 4:
                    small_out[...] = total
                    sm_send[4] = total
                    small(4).start()
                else:
                    small_out[5:7] = total[5:7]

        @at("branch_near")
        def _():
            branch_near()

        @at("finish")
        def _():
            finish()

        return 0

    lax.fori_loop(0, len(TURNS) * (waves + 5), turn_of, 0)

    def drain(w, _):
        cp("A5", w).wait_send()
        cp("G", w).wait()
        local(w).wait()

        @pl.when(inner)
        def _():
            for k in ("A4", "B4", "B5a", "B5b"):
                cp(k, w).wait_send()

        return 0

    lax.fori_loop(0, waves, drain, 0)
    p_ff(n_ff - 2).wait_send()
    p_ff(n_ff - 1).wait_send()
    for i in range(n_rb):
        xcopy(0, i).wait_send()
        xcopy(1, i).wait_send()
    for i in range(n_rb - 1):
        r_copy(i, x).wait_send()
    for i in range(n_g):
        g_copy(i).wait_send()
    for i in range(5):
        small(i).wait_send()
    out_copy().wait()
    pltpu.make_async_copy(acc, grad_in, out_sem.at[1]).wait()


def mega(g_n, r_n, w_qkv, wo, w_up, w_down, *small):
    half, width = g_n.shape
    rows = 2 * half
    hidden = w_down.shape[0]
    heads = wo.shape[0] // HD
    n_g = width // RW
    waves = 2 * n_g + heads // 2
    n_rb = half // 256
    vm = pl.BlockSpec(memory_space=pltpu.VMEM)
    hbm = pl.BlockSpec(memory_space=pl.ANY)
    dma = pltpu.SemaphoreType.DMA
    v16 = lambda *s: pltpu.VMEM(s, bf16)
    v32 = lambda *s: pltpu.VMEM(s, f32)
    return pl.pallas_call(
        functools.partial(mega_kernel, heads),
        in_specs=[hbm] * 6 + [vm] * len(small),
        out_specs=[hbm, hbm, hbm, vm],
        out_shape=[
            jax.ShapeDtypeStruct((waves, 2 * RW, width), bf16),
            jax.ShapeDtypeStruct((half, width), bf16),
            jax.ShapeDtypeStruct((half, width), f32),
            jax.ShapeDtypeStruct((8, width), f32),
        ],
        scratch_shapes=[
            v16(rows, hidden), v16(rows, hidden), v16(rows, width), v16(rows, width), v16(rows, width),
            v16(heads * 3 * HD, width), v16(heads * HD, width), v16(width, hidden), v16(hidden, width),
            v16(waves, RW, width), v16(2, 2, RW, width), v16(NP, 2, RW, width),
            v16(NS, RQ, width), v16(NS, RQ, width), v16(NS, RQ, width), v16(NS, 2 * RQ, width), v16(NS, RQ, width), v16(NS, RQ, width),
            v32(6 * HD, rows), v16(2 * HD, rows), v16(heads * 3 * HD, rows), v16(heads * HD, rows), v16(RW, rows),
            v16(256, heads * 3 * HD), v32(half, width),
            v32(5, 8, width), v32(5, 8, width), v32(8, width),
            dma((len(KINDS), waves)), dma((len(KINDS), waves)), dma((waves,)), dma((N_LOADS,)), dma((n_rb,)), dma((n_rb,)),
            dma((n_g,)), dma((n_g,)), dma((2, n_rb)), dma((2, n_rb)), dma((5,)), dma((5,)), dma((2,))] + [pltpu.SemaphoreType.REGULAR] * 4,
        compiler_params=pltpu.CompilerParams(collective_id=0, has_side_effects=True, vmem_limit_bytes=63 * 2**20),
        name="attention_and_sums",
    )(g_n, r_n, w_qkv, wo, w_up, w_down, *small)


def widen_kernel(
    n_g, n_at, src, out_in, grad_in, small, down, up, qkv, proj, out, grad, g_gain, g_bias, g_qkv, g_out, g_down, g_up,
    buf, wide, wide_q, wide_p, buf_o, buf_g, in_sem, sem, q_sem, p_sem, through_sem,
):
    waves, _, width = src.shape
    hq = 3 * HD
    arrive = [pltpu.make_async_copy(a, b, through_sem.at[i]) for i, (a, b) in enumerate(((out_in, buf_o), (grad_in, buf_g)))]
    leave = [pltpu.make_async_copy(a, b, through_sem.at[2 + i]) for i, (a, b) in enumerate(((buf_o, out), (buf_g, grad)))]
    loads = [pltpu.make_async_copy(src.at[w], buf.at[w], in_sem.at[w]) for w in range(waves)]
    for k in arrive + loads:
        k.start()
    row = lax.broadcasted_iota(jnp.int32, (RW, RW), 0)
    eye = jnp.where(row == lax.broadcasted_iota(jnp.int32, (RW, RW), 1), 1.0, 0.0).astype(bf16)
    slots, busy, used = wide.shape[0], {}, 0
    for a, b in zip(arrive, leave):
        a.wait()
        b.start()

    def free(slot):
        for k in busy.pop(slot, []):
            k.wait()

    def send(slot, copies):
        for k in copies:
            k.start()
        busy[slot] = copies

    for w in range(waves):
        loads[w].wait()
        if n_g <= w < n_g + n_at:
            j = w - n_g
            s = j % 2
            free(("q", s))
            for k in range(width // RW):
                cols = slice(k * RW, (k + 1) * RW)
                both = jnp.concatenate([buf[w, 0:hq, cols], buf[w, RW : RW + hq, cols]], axis=0)
                wide_q[s, cols] = dot_nt(eye, both)
            for c in range(2):
                wide_p[s, c * HD : (c + 1) * HD] = buf[w, c * RW + hq : (c + 1) * RW].astype(f32)
            send(("q", s), [
                pltpu.make_async_copy(wide_q.at[s], qkv.at[:, pl.ds(j * 2 * hq, 2 * hq)], q_sem.at[s]),
                pltpu.make_async_copy(wide_p.at[s], proj.at[pl.ds(j * 2 * HD, 2 * HD)], p_sem.at[s]),
            ])
            continue
        s = used % slots
        used += 1
        free(s)
        copies = []
        for c in range(2):
            if w < n_g:
                for k in range(width // RW):
                    n = c * (width // RW) + k
                    cols = slice(n * RW, (n + 1) * RW)
                    wide[s, :, cols] = dot_nt(eye, buf[w, c * RW : (c + 1) * RW, k * RW : (k + 1) * RW])
                    copies.append(
                        pltpu.make_async_copy(
                            wide.at[s, :, cols], down.at[cols, pl.ds(w * RW, RW)], sem.at[s, n]
                        )
                    )
            else:
                wide[s, :, c * width : (c + 1) * width] = buf[w, c * RW : (c + 1) * RW].astype(f32)
        if w >= n_g:
            copies = [pltpu.make_async_copy(wide.at[s], up.at[pl.ds((w - n_g - n_at) * RW, RW)], sem.at[s, 0])]
        send(s, copies)
    n_up = g_up.shape[0] // width
    for i in range(n_up):
        g_up[i * width : (i + 1) * width] = small[i]
    g_out[...] = small[n_up]
    g_down[...] = small[n_up]
    g_qkv[0:width] = small[3]
    g_qkv[width:] = small[4, 0 : g_qkv.shape[0] - width]
    g_gain[...] = small[5]
    g_bias[...] = small[6]
    for s in list(busy):
        free(s)
    for k in leave:
        k.wait()


def widen(red, out, grad_in, small, hidden):
    waves, _, width = red.shape
    n_g = width // RW
    n_at = waves - 2 * n_g
    vm = pl.BlockSpec(memory_space=pltpu.VMEM)
    hbm = pl.BlockSpec(memory_space=pl.ANY)
    dma = pltpu.SemaphoreType.DMA
    s32 = lambda *s: jax.ShapeDtypeStruct(s, f32)
    return pl.pallas_call(
        functools.partial(widen_kernel, n_g, n_at),
        in_specs=[hbm] * 3 + [vm],
        out_specs=[hbm] * 6 + [vm] * 6,
        out_shape=[
            s32(hidden, width), s32(width, hidden), s32(width, n_at * 6 * HD), s32(n_at * 2 * HD, width),
            jax.ShapeDtypeStruct(out.shape, out.dtype), s32(*grad_in.shape),
            s32(width), s32(width), s32(n_at * 6 * HD), s32(width), s32(width), s32(hidden),
        ],
        scratch_shapes=[
            pltpu.VMEM((waves, 2 * RW, width), bf16), pltpu.VMEM((4, RW, hidden), f32), pltpu.VMEM((2, width, 6 * HD), f32),
            pltpu.VMEM((2, 2 * HD, width), f32), pltpu.VMEM(out.shape, out.dtype), pltpu.VMEM(grad_in.shape, f32),
            dma((waves,)), dma((4, hidden // RW)), dma((2,)), dma((2,)), dma((4,)),
        ],
        compiler_params=pltpu.CompilerParams(vmem_limit_bytes=56 * 2**20),
        name="widen",
    )(red, out, grad_in, small)


def shards(residual, ln_gain, ln_bias, w_qkv, b_qkv, w_out, b_out, w_up, b_up, w_down, b_down, grad_out):
    rows = 2 * residual.shape[0]
    half_rot = ROT // 2
    inverse = 1.0 / np.float32(10000.0) ** (np.arange(half_rot, dtype=np.float32) * np.float32(2.0 / ROT))
    angles = np.arange(rows, dtype=np.float32)[None, :] * inverse[:, None].astype(np.float32)
    cs = jnp.asarray(np.concatenate([np.cos(angles), np.sin(angles)]).astype(np.float32))
    red, out, grad_in, small = mega(
        grad_out, residual, w_qkv, w_out, w_up, w_down, b_qkv, b_up, cs, ln_gain, ln_bias, b_out, b_down
    )
    grad_w_down, grad_w_up, grad_w_qkv, grad_w_out, out, grad_in, gain, bias, gb_qkv, gb_out, gb_down, gb_up = widen(
        red, out, grad_in, small, w_down.shape[0]
    )
    return out, grad_in, gain, bias, grad_w_qkv, gb_qkv, grad_w_out, gb_out, grad_w_up, gb_up, grad_w_down, gb_down


def contract_rows(left, right):
    return lax.dot_general(
        left, right, (((0,), (0,)), ((), ())), preferred_element_type=jnp.float32
    )


def contract_cols(left, right):
    return lax.dot_general(
        left, right, (((1,), (1,)), ((), ())), preferred_element_type=jnp.float32
    )


def turn_heads(heads, cosine, sine):
    half_rot = ROT // 2
    first = heads[:, :, :half_rot]
    second = heads[:, :, half_rot:ROT]
    rest = heads[:, :, ROT:]
    cos_rows = cosine[:, None, :]
    sin_rows = sine[:, None, :]
    return jnp.concatenate(
        [first * cos_rows - second * sin_rows, second * cos_rows + first * sin_rows, rest], axis=2
    )


def undo_turn(heads, cosine, sine):
    half_rot = ROT // 2
    first = heads[:, :, :half_rot]
    second = heads[:, :, half_rot:ROT]
    rest = heads[:, :, ROT:]
    cos_rows = cosine[:, None, :]
    sin_rows = sine[:, None, :]
    return jnp.concatenate(
        [first * cos_rows + second * sin_rows, second * cos_rows - first * sin_rows, rest], axis=2
    )


def shards_any(
    residual, ln_gain, ln_bias, w_qkv, b_qkv, w_out, b_out, w_up, b_up, w_down, b_down, grad_out
):
    rows_here = residual.shape[0]
    head_cols = w_out.shape[0]
    heads_here = head_cols // HD
    resid_wide = residual.astype(jnp.float32)
    average = jnp.mean(resid_wide, axis=1, keepdims=True)
    centered = resid_wide - average
    variance = jnp.mean(centered * centered, axis=1, keepdims=True)
    inv_std = lax.rsqrt(variance + epsilon)
    normed = centered * inv_std
    h_local = (normed * ln_gain + ln_bias).astype(jnp.bfloat16)
    h_full = lax.all_gather(h_local, "tensor", axis=0, tiled=True)
    group_rows = h_full.shape[0]
    seqlen = min(LEN_MAX, group_rows)
    seq_count = group_rows // seqlen
    qkv = jnp.dot(h_full, w_qkv, preferred_element_type=jnp.float32) + b_qkv
    up_lin = jnp.dot(h_full, w_up, preferred_element_type=jnp.float32) + b_up
    act_wide, gelu_back = jax.vjp(functools.partial(jax.nn.gelu, approximate=False), up_lin)
    act = act_wide.astype(jnp.bfloat16)
    cosine, sine = turn_tables(seqlen)
    causal = jnp.arange(seqlen)[:, None] >= jnp.arange(seqlen)[None, :]
    scale = 1.0 / math.sqrt(HD)

    def attend(block):
        queries = turn_heads(block[:, :, 0, :], cosine, sine).astype(jnp.bfloat16)
        key_rows = turn_heads(block[:, :, 1, :], cosine, sine).astype(jnp.bfloat16)
        value_rows = block[:, :, 2, :].astype(jnp.bfloat16)
        scores = (
            jnp.einsum("qhd,khd->hqk", queries, key_rows, preferred_element_type=jnp.float32)
            * scale
        )
        scores = jnp.where(causal[None], scores, -1e30)
        peak = jnp.max(scores, axis=2, keepdims=True)
        raised = jnp.exp(scores - peak)
        totals = jnp.sum(raised, axis=2, keepdims=True)
        probs = raised / totals
        attended = jnp.einsum(
            "hqk,khd->qhd",
            probs.astype(jnp.bfloat16),
            value_rows,
            preferred_element_type=jnp.float32,
        ).astype(jnp.bfloat16)
        log_total = peak[:, :, 0] + jnp.log(totals[:, :, 0])
        return (queries, key_rows, value_rows, attended, log_total)

    blocks = qkv.reshape(seq_count, seqlen, heads_here, 3, HD)
    queries, key_rows, value_rows, attended, log_total = lax.map(attend, blocks)
    attn_rows = attended.reshape(group_rows, head_cols)
    act_part = lax.slice_in_dim(act, 0, lax.axis_size("tensor") * rows_here, axis=0)
    branch = lax.psum_scatter(
        jnp.dot(attn_rows, w_out, preferred_element_type=jnp.float32)
        + jnp.dot(act_part, w_down, preferred_element_type=jnp.float32),
        "tensor",
        scatter_dimension=0,
        tiled=True,
    )
    out = (resid_wide + branch + b_out + b_down).astype(jnp.bfloat16)
    grad_local = grad_out.astype(jnp.float32)
    grad_full = lax.all_gather(grad_out, "tensor", axis=0, tiled=True)
    grad_w_out = contract_rows(attn_rows, grad_full)
    grad_w_down = contract_rows(act, grad_full)
    d_attended = contract_cols(grad_full, w_out).astype(jnp.bfloat16)
    d_act = contract_cols(grad_full, w_down)
    d_up = gelu_back(d_act)[0].astype(jnp.bfloat16)
    grad_b_up = jnp.sum(d_up, axis=0, dtype=jnp.float32)

    def attend_back(items):
        query_part, key_part, value_part, log_part, d_part = items
        scores = (
            jnp.einsum("qhd,khd->hqk", query_part, key_part, preferred_element_type=jnp.float32)
            * scale
        )
        probs = jnp.where(causal[None], jnp.exp(scores - log_part[:, :, None]), 0.0)
        grad_values = jnp.einsum(
            "hqk,qhd->khd", probs.astype(jnp.bfloat16), d_part, preferred_element_type=jnp.float32
        )
        d_probs = jnp.einsum("qhd,khd->hqk", d_part, value_part, preferred_element_type=jnp.float32)
        d_scores = (probs * (d_probs - jnp.sum(d_probs * probs, axis=2, keepdims=True))).astype(
            jnp.bfloat16
        )
        d_query = (
            jnp.einsum("hqk,khd->qhd", d_scores, key_part, preferred_element_type=jnp.float32)
            * scale
        )
        d_key = (
            jnp.einsum("hqk,qhd->khd", d_scores, query_part, preferred_element_type=jnp.float32)
            * scale
        )
        return jnp.stack(
            [undo_turn(d_query, cosine, sine), undo_turn(d_key, cosine, sine), grad_values], axis=2
        )

    d_blocks = d_attended.reshape(seq_count, seqlen, heads_here, HD)
    d_qkv = lax.map(attend_back, (queries, key_rows, value_rows, log_total, d_blocks))
    d_qkv = d_qkv.reshape(group_rows, 3 * head_cols).astype(jnp.bfloat16)
    grad_b_qkv = jnp.sum(d_qkv, axis=0, dtype=jnp.float32)
    grad_w_qkv = contract_rows(h_full, d_qkv)
    grad_w_up = contract_rows(h_full, d_up)
    d_hidden = lax.psum_scatter(
        contract_cols(d_qkv, w_qkv) + contract_cols(d_up, w_up),
        "tensor",
        scatter_dimension=0,
        tiled=True,
    )
    gain_local = jnp.sum(d_hidden * normed, axis=0)
    bias_local = jnp.sum(d_hidden, axis=0)
    d_hat = d_hidden * ln_gain
    grad_in = grad_local + inv_std * (
        d_hat
        - jnp.mean(d_hat, axis=1, keepdims=True)
        - normed * jnp.mean(d_hat * normed, axis=1, keepdims=True)
    )
    out_bias = jnp.sum(grad_full, axis=0, dtype=jnp.float32)
    grad_w_qkv, grad_b_qkv, grad_w_out, grad_w_up, grad_b_up, grad_w_down, grad_b_out = lax.psum(
        (grad_w_qkv, grad_b_qkv, grad_w_out, grad_w_up, grad_b_up, grad_w_down, out_bias), "dp"
    )
    grad_ln_gain, grad_ln_bias = lax.psum((gain_local, bias_local), ("dp", "tensor"))
    return (
        out,
        grad_in,
        grad_ln_gain,
        grad_ln_bias,
        grad_w_qkv,
        grad_b_qkv,
        grad_w_out,
        grad_b_out,
        grad_w_up,
        grad_b_up,
        grad_w_down,
        grad_b_out,
    )


def solution(mesh):
    small_slice = mesh.shape["dp"] == 16 and mesh.shape["tensor"] == 2
    return jax.shard_map(
        shards if small_slice else shards_any,
        mesh=mesh,
        in_specs=(
            P(("dp", "tensor"), None),
            P(),
            P(),
            P(None, "tensor"),
            P("tensor"),
            P("tensor", None),
            P(),
            P(None, "tensor"),
            P("tensor"),
            P("tensor", None),
            P(),
            P(("dp", "tensor"), None),
        ),
        out_specs=(
            P(("dp", "tensor"), None),
            P(("dp", "tensor"), None),
            P(),
            P(),
            P(None, "tensor"),
            P("tensor"),
            P("tensor", None),
            P(),
            P(None, "tensor"),
            P("tensor"),
            P("tensor", None),
            P(),
        ),
        check_vma=False,
    )
```

```python
import functools
import math

import jax
import jax.numpy as jnp
import numpy as np
from jax import lax
from jax.experimental import pallas as pl
from jax.experimental.pallas import tpu as pltpu
from jax.sharding import PartitionSpec as P

HD = 64
ROT = 16
LEN_MAX = 1024
epsilon = 1e-05
MESH = pl.DeviceIdType.MESH
f32 = jnp.float32
bf16 = jnp.bfloat16


def dot(left, right):
    return lax.dot_general(left, right, (((1,), (0,)), ((), ())), preferred_element_type=f32)


def dot_nt(left, right):
    return lax.dot_general(left, right, (((1,), (1,)), ((), ())), preferred_element_type=f32)


def turn_tables(seqlen):
    half_rot = ROT // 2
    exponent = jnp.arange(half_rot, dtype=f32) * (2.0 / ROT)
    inverse = 1.0 / 10000.0**exponent
    places = jnp.arange(seqlen, dtype=f32)
    angles = places[:, None] * inverse[None, :]
    return (jnp.cos(angles), jnp.sin(angles))


def turn(t, cos, sin, sign):
    a, b = t[0:8], t[8:16]
    return jnp.concatenate([a * cos - sign * (b * sin), b * cos + sign * (a * sin), t[16:]], axis=0)


def attend_head(q_t, k_t, v_t, do_t, cos, sin, blk=256):
    seq = q_t.shape[1]
    nb = seq // blk
    qs = turn(q_t, cos, sin, 1.0).astype(bf16) * jnp.asarray(0.125, bf16)
    kb = turn(k_t, cos, sin, 1.0).astype(bf16)
    vb = v_t.astype(bf16)
    keys, values, queries, grads = kb.T, vb.T, qs.T, do_t.T
    seen = lax.broadcasted_iota(jnp.int32, (blk, blk), 0) <= lax.broadcasted_iota(jnp.int32, (blk, blk), 1)
    outs, dqs, dv_sum, dk_sum = [], [], [None] * nb, [None] * nb

    def products(i):
        kk, sl = (i + 1) * blk, slice(i * blk, (i + 1) * blk)
        return dot(keys[:kk], qs[:, sl]), dot(values[:kk], do_t[:, sl])

    def gather(sums, i, v):
        for j in range(i + 1):
            a = v[j * blk : (j + 1) * blk]
            sums[j] = a if sums[j] is None else sums[j] + a

    def back(i, p, dp):
        kk, sl = (i + 1) * blk, slice(i * blk, (i + 1) * blk)
        ds = (p * (dp - jnp.sum(p * dp, axis=0, keepdims=True))).astype(bf16)
        dqs.append(dot(kb[:, :kk], ds) * 0.125)
        gather(dk_sum, i, dot(ds, queries[sl]))

    ahead, behind = products(0), None
    for i in range(nb):
        kk, sl = (i + 1) * blk, slice(i * blk, (i + 1) * blk)
        s, dp = ahead
        if i + 1 < nb:
            ahead = products(i + 1)
        diag = jnp.where(seen, s[i * blk :], -1e30)
        s = jnp.concatenate([s[: i * blk], diag], axis=0) if i else diag
        p = jnp.exp(s - jnp.max(s, axis=0, keepdims=True))
        p = p * (1.0 / jnp.sum(p, axis=0, keepdims=True))
        pb = p.astype(bf16)
        outs.append(dot(vb[:, :kk], pb).astype(bf16))
        gather(dv_sum, i, dot(pb, grads[sl]))
        if behind is not None:
            back(*behind)
        behind = (i, p, dp)
    back(*behind)
    dq_t = turn(jnp.concatenate(dqs, axis=1), cos, sin, -1.0)
    dk_t = turn(jnp.concatenate(dk_sum, axis=0).T, cos, sin, -1.0)
    dv_t = jnp.concatenate(dv_sum, axis=0).T
    return jnp.concatenate(outs, axis=1), dq_t, dk_t, dv_t


def gelu_and_slope(u):
    half = 0.5 + 0.5 * lax.erf(u * (1.0 / math.sqrt(2.0)))
    bell = jnp.exp(u * u * -0.5) * (1.0 / math.sqrt(2.0 * math.pi))
    return u * half, half + u * bell


RW = 256
RQ = RW // 4
NS = 4
NP = 2
KINDS = ("P", "A1", "A2", "A3", "A4", "A5", "B1", "B2", "B3", "B4", "B5a", "B5b", "G")
KI = {k: i for i, k in enumerate(KINDS)}
TURNS = ((6, 5, 4), (3, 2, 1), ())
FF_AT = (1, 4, 7, 22, 24, 27, 30)
HEAD_AT = (8, 9, 10, 12, 13, 15, 16, 18)
PLAN = {
    "branch_ff": 5, "free": 12, "d_up": 19, "branch_far": 21, "back_far": 25, "back_near": 28, "small": 31,
    "branch_near": 36, "finish": 45,
}
SMALL_AT = (34, 37, 40, 43, 46)
BC = 512
WC = 256
N_LOADS = 6


def mega_kernel(
    heads,
    g_n, r_n, w_qkv, wo, w_up, w_down, bq, bu, cs, ln_gain, ln_bias, b_out, b_down,
    red, out, grad_in, small_out,
    act2, dup2, h2, g2, r2, w_t2, wo2, w_up2, w_dn2, x_buf, fw, ag, ra1, ra2, ra3, rb1, rb2, rb3,
    qkv_s, do_s, dqkv_t, att_t, t_buf, tq, acc,
    sm_send, sm_recv, sums,
    ss, rs, loc_sem, load_sem, r_ss, r_rs, g_ss, g_rs, x_ss, x_rs, sm_ss, sm_rs, out_sem, free_sem, y_free, z_free, m_free,
):
    half, width = g_n.shape
    hidden = w_down.shape[0]
    n_g = width // RW
    n_at = heads // 2
    n_ff = 2 * n_g
    waves = n_ff + n_at
    first_up = n_g + n_at
    dp, x = lax.axis_index("dp"), lax.axis_index("tensor")
    c, y, z = lax.rem(dp, 2), lax.rem(dp // 2, 2), dp // 4
    dev = lambda zz, yy, cc, xx: (zz * 4 + yy * 2 + cc, xx)
    sib = dev(z, y, 1 - c, x)
    yp = dev(z, 1 - y, c, x)
    zp = dev(z + 1 - 2 * lax.rem(z, 2), y, c, x)
    zm = dev(3 - z, y, c, x)
    xp = dev(z, y, c, 1 - x)
    inner = jnp.logical_or(z == 1, z == 2)
    outer = jnp.logical_not(inner)
    near = pl.ds(pl.multiple_of(x * half, half), half)
    far = pl.ds(pl.multiple_of((1 - x) * half, half), half)

    loads = []
    staged = act2.at[:, pl.ds(0, w_qkv.shape[1])]
    for src, dst in (
        (w_qkv, staged), (r_n, r2.at[near]), (w_up, w_up2), (g_n, g2.at[near]), (w_down, w_dn2), (wo, wo2),
    ):
        loads.append(pltpu.make_async_copy(src, dst, load_sem.at[len(loads)]))
    for k in loads:
        k.start()

    barrier = pltpu.get_barrier_semaphore()
    for d in (xp, sib, yp, zp, zm):
        pl.semaphore_signal(barrier, inc=1, device_id=d, device_id_type=MESH)
    pl.semaphore_wait(barrier, 5)

    def g_copy(i):
        cols = pl.ds(pl.multiple_of(i * RW, RW), RW)
        return pltpu.make_async_remote_copy(
            src_ref=g_n.at[:, cols], dst_ref=g2.at[near, cols], send_sem=g_ss.at[i], recv_sem=g_rs.at[i],
            device_id=xp, device_id_type=MESH,
        )

    def g_arrives(i):
        cols = pl.ds(pl.multiple_of(i * RW, RW), RW)
        pltpu.make_async_remote_copy(
            src_ref=g_n.at[:, cols], dst_ref=g2.at[far, cols], send_sem=g_ss.at[i], recv_sem=g_rs.at[i],
            device_id=xp, device_id_type=MESH,
        ).wait_recv()

    rb = 256
    n_rb = half // rb

    def rows_of(who, i):
        return pl.ds(pl.multiple_of(who * half + i * rb, rb), rb)

    def r_copy(i, who):
        return pltpu.make_async_remote_copy(
            src_ref=r_n.at[pl.ds(pl.multiple_of(i * rb, rb), rb)], dst_ref=r2.at[rows_of(who, i)],
            send_sem=r_ss.at[i], recv_sem=r_rs.at[i], device_id=xp, device_id_type=MESH,
        )

    for i in range(n_rb):
        r_copy(i, x).start()


    a_mine = pl.ds(pl.multiple_of(y * RQ, RQ), RQ)
    a_other = pl.ds(pl.multiple_of((1 - y) * RQ, RQ), RQ)
    zi = jnp.where(z == 2, 1, 0)
    b_mine = pl.ds(pl.multiple_of(2 * RQ + zi * RQ, RQ), RQ)
    b_other = pl.ds(pl.multiple_of(2 * RQ + (1 - zi) * RQ, RQ), RQ)
    b_all = pl.ds(2 * RQ, 2 * RQ)

    def rc(kind, w, src, dst, device):
        k = KI[kind]
        return pltpu.make_async_remote_copy(
            src_ref=src, dst_ref=dst, send_sem=ss.at[k, w], recv_sem=rs.at[k, w], device_id=device, device_id_type=MESH
        )

    def cp(kind, w):
        s = lax.rem(w, NS)
        if kind == "A1":
            return rc(kind, w, x_buf.at[w, a_other], ra1.at[s], yp)
        if kind == "A2":
            return rc(kind, w, x_buf.at[w, a_mine], ra2.at[s], zp)
        if kind == "A3":
            return rc(kind, w, x_buf.at[w, a_mine], ra3.at[s], zm)
        if kind == "A4":
            return rc(kind, w, x_buf.at[w, a_mine], x_buf.at[w, a_mine], zp)
        if kind == "A5":
            return rc(kind, w, x_buf.at[w, a_mine], x_buf.at[w, a_mine], yp)
        if kind == "B1":
            return rc(kind, w, x_buf.at[w, b_all], rb1.at[s], zp)
        if kind == "B2":
            return rc(kind, w, x_buf.at[w, b_other], rb2.at[s], zm)
        if kind == "B3":
            return rc(kind, w, x_buf.at[w, b_mine], rb3.at[s], yp)
        if kind == "B4":
            return rc(kind, w, x_buf.at[w, b_mine], x_buf.at[w, b_mine], zm)
        if kind == "B5a":
            return rc(kind, w, x_buf.at[w, b_mine], x_buf.at[w, b_mine], zp)
        if kind == "B5b":
            return rc(kind, w, x_buf.at[w, b_other], x_buf.at[w, b_other], zp)
        if kind == "G":
            there = red.at[w, pl.ds(pl.multiple_of(c * RW, RW), RW)]
            return rc(kind, w, x_buf.at[w], there, sib)

    def wave_of(k):
        return jnp.where(k < n_g, k, k + n_at)

    def p_ff(k):
        return rc("P", wave_of(k), fw.at[lax.rem(k, 2), 1 - c], x_buf.at[wave_of(k)], sib)

    def p_at(j):
        return rc("P", n_g + j, ag.at[lax.rem(j, NP), 1 - c], x_buf.at[n_g + j], sib)

    def local(w):
        here = red.at[w, pl.ds(pl.multiple_of(c * RW, RW), RW)]
        return pltpu.make_async_copy(x_buf.at[w], here, loc_sem.at[w])

    def add(a, b):
        return (a.astype(f32) + b.astype(f32)).astype(bf16)

    def give(sem, device):
        pl.semaphore_signal(sem, inc=1, device_id=device, device_id_type=MESH)

    def stage(s, t):
        w = t - (s - 1)
        ok = jnp.logical_and(w >= 0, w < waves)
        slot = lax.rem(w, NS)
        if s == 1:

            of_heads = jnp.logical_and(w >= n_g, w < first_up)

            @pl.when(jnp.logical_and(ok, jnp.logical_not(of_heads)))
            def _():
                k = jnp.where(w < n_g, w, w - n_at)
                p_ff(k).wait_recv()
                x_buf[w] = add(x_buf[w], fw[lax.rem(k, 2), c])

            @pl.when(jnp.logical_and(ok, of_heads))
            def _():
                p_at(w - n_g).wait_recv()
                x_buf[w] = add(x_buf[w], ag[lax.rem(w - n_g, NP), c])

            @pl.when(ok)
            def _():
                cp("A1", w).start()

                @pl.when(outer)
                def _():
                    cp("B1", w).start()

        if s == 2:

            @pl.when(ok)
            def _():
                cp("A1", w).wait()
                give(y_free, yp)
                x_buf[w, a_mine] = add(x_buf[w, a_mine], ra1[slot])

                @pl.when(outer)
                def _():
                    cp("A2", w).start()

                @pl.when(inner)
                def _():
                    cp("B1", w).wait_recv()
                    x_buf[w, b_all] = add(x_buf[w, b_all], rb1[slot])
                    cp("B2", w).start()

        if s == 3:

            @pl.when(jnp.logical_and(ok, outer))
            def _():
                cp("B1", w).wait_send()
                cp("A2", w).wait_send()
                give(z_free, zp)

            @pl.when(jnp.logical_and(ok, inner))
            def _():
                cp("A2", w).wait_recv()
                x_buf[w, a_mine] = add(x_buf[w, a_mine], ra2[slot])
                cp("A3", w).start()
                cp("B2", w).wait()
                give(m_free, zm)
                x_buf[w, b_mine] = add(x_buf[w, b_mine], rb2[slot])
                cp("B3", w).start()

        if s == 4:

            @pl.when(jnp.logical_and(ok, inner))
            def _():
                cp("A3", w).wait()
                x_buf[w, a_mine] = add(x_buf[w, a_mine], ra3[slot])
                pl.semaphore_wait(z_free, 1)
                cp("A4", w).start()
                pl.semaphore_wait(y_free, 1)
                cp("A5", w).start()
                cp("B3", w).wait()
                x_buf[w, b_mine] = add(x_buf[w, b_mine], rb3[slot])
                pl.semaphore_wait(m_free, 1)
                cp("B4", w).start()
                cp("B5a", w).start()

        if s == 5:

            @pl.when(jnp.logical_and(ok, inner))
            def _():
                cp("B4", w).wait_recv()
                cp("B5b", w).start()

            @pl.when(jnp.logical_and(ok, outer))
            def _():
                cp("A4", w).wait_recv()
                pl.semaphore_wait(y_free, 1)
                cp("A5", w).start()

        if s == 6:

            @pl.when(ok)
            def _():
                cp("A5", w).wait_recv()

                @pl.when(outer)
                def _():
                    cp("B5a", w).wait_recv()
                    cp("B5b", w).wait_recv()

                cp("G", w).start()
                local(w).start()


    def ff_wave(k):
        @pl.when(k >= 2)
        def _():
            p_ff(k - 2).wait_send()

        def product(src, full):
            t_buf[...] = src.T

            def block(n, _):
                cols = pl.ds(pl.multiple_of(n * BC, BC), BC)
                per = width // BC
                fw[lax.rem(k, 2), n // per, :, pl.ds(pl.multiple_of(lax.rem(n, per) * BC, BC), BC)] = dot(
                    t_buf[...], full[:, cols]
                ).astype(bf16)
                return 0

            lax.fori_loop(0, hidden // BC, block, 0)

        @pl.when(k < n_g)
        def _():
            g_arrives(k)
            product(g2[:, pl.ds(pl.multiple_of(k * RW, RW), RW)], act2)

        @pl.when(k >= n_g)
        def _():
            product(h2[:, pl.ds(pl.multiple_of((k - n_g) * RW, RW), RW)], dup2)

        p_ff(k).start()

    n_hid = hidden // WC

    def norm(rows):
        r = r2[rows].astype(f32)
        centered = r - jnp.mean(r, axis=1, keepdims=True)
        inv = lax.rsqrt(jnp.mean(centered * centered, axis=1, keepdims=True) + epsilon)
        return r, centered * inv, inv

    def make_hidden(rows):
        h2[rows] = (norm(rows)[1] * ln_gain[...][None] + ln_bias[...][None]).astype(bf16)

    def turn_weights():
        def body(n, _):
            here = pl.ds(pl.multiple_of(n * WC, WC), WC)
            w_t2[here] = act2[:, here].T
            return 0

        lax.fori_loop(0, w_qkv.shape[1] // WC, body, 0)

    def over(total, size, body):
        def step(n, _):
            body(pl.ds(pl.multiple_of(n * size, size), size))
            return 0

        lax.fori_loop(0, total // size, step, 0)

    def ff_near():
        def body(cols):
            a, slope = gelu_and_slope(dot(h2[near], w_up2[:, cols]) + bu[cols][None])
            act2[near, cols] = a.astype(bf16)
            dup2[near, cols] = (dot_nt(g2[near], w_dn2[cols]) * slope).astype(bf16)

        over(hidden, WC, body)

    def ff_far(i):
        r = rows_of(1 - x, i)
        r_copy(i, 1 - x).wait_recv()
        make_hidden(r)

        def body(cols):
            a, slope = gelu_and_slope(dot(h2[r], w_up2[:, cols]) + bu[cols][None])
            act2[r, cols] = a.astype(bf16)
            dup2[r, cols] = slope.astype(bf16)

        over(hidden, BC, body)

    def d_up_far():
        def body(cols):
            dup2[far, cols] = (dot_nt(g2[far], w_dn2[cols]) * dup2[far, cols].astype(f32)).astype(bf16)

        over(hidden, WC, body)


    cos, sin = cs[0:8], cs[8:16]
    hq, hv = 3 * HD, HD

    def head(t):
        odd = lax.rem(t, 2)
        j = t // 2
        pair_q = pl.ds(pl.multiple_of(j * 2 * hq, 2 * HD), 2 * hq)
        pair_v = pl.ds(pl.multiple_of(j * 2 * hv, 2 * HD), 2 * hv)

        @pl.when(odd == 0)
        def _():
            bias = jnp.broadcast_to(bq[pl.ds(pl.multiple_of(j * 2 * hq, 128), 2 * hq)][None], (128, 2 * hq)).T
            qkv_s[...] = dot_nt(w_t2[pair_q], h2[...]) + bias[:, 0:1]
            do_s[...] = dot_nt(wo2[pair_v], g2[...]).astype(bf16)

        part = lambda i: qkv_s[pl.ds(pl.multiple_of(odd * hq + i * HD, HD), HD)]
        o, dq, dk, dv = attend_head(
            part(0), part(1), part(2), do_s[pl.ds(pl.multiple_of(odd * hv, HD), HD)], cos, sin
        )
        att_t[pl.ds(pl.multiple_of(t * hv, HD), HD)] = o
        for i, v in enumerate((dq, dk, dv)):
            dqkv_t[pl.ds(pl.multiple_of(t * hq + i * HD, HD), HD)] = v.astype(bf16)

        @pl.when(odd == 1)
        def _():
            slot = lax.rem(j, NP)

            @pl.when(j >= NP)
            def _():
                p_at(j - NP).wait_send()

            gq = dot(dqkv_t[pair_q], h2[...]).astype(bf16)
            gv = dot(att_t[pair_v], g2[...]).astype(bf16)
            for i in range(2):
                ag[slot, i, 0:hq] = gq[i * hq : (i + 1) * hq]
                ag[slot, i, hq : hq + hv] = gv[i * hv : (i + 1) * hv]
            p_at(j).start()


    def xcopy(which, i):
        there = act2.at[rows_of(x, i), pl.ds(which * width, width)]
        return pltpu.make_async_remote_copy(
            src_ref=ag.at[which, i], dst_ref=there, send_sem=x_ss.at[which, i], recv_sem=x_rs.at[which, i],
            device_id=xp, device_id_type=MESH,
        )

    def arrived(which, i):
        return act2.at[rows_of(1 - x, i), pl.ds(which * width, width)]

    def each(body):
        def step(i, _):
            body(i, pl.ds(pl.multiple_of(i * rb, rb), rb))
            return 0

        lax.fori_loop(0, n_rb, step, 0)

    def branch_ff_far():
        def body(cols):
            acc[:, cols] = dot(act2[far], w_dn2[:, cols])

        over(width, WC, body)

    def back(who):
        def rows(i, here):
            r = rows_of(who, i)
            tq[...] = dqkv_t[:, r].T
            _, normed, _ = norm(r)

            def body(cols):
                acc[here, cols] = dot(tq[...], w_t2[:, cols]) + dot_nt(dup2[r], w_up2[cols])

            over(width, WC, body)
            d = acc[here]
            sums[0:1] = sums[0:1] + jnp.sum(d * normed, axis=0, keepdims=True)
            sums[1:2] = sums[1:2] + jnp.sum(d, axis=0, keepdims=True)
            if who is not x:
                ag[1, i] = d.astype(bf16)
                xcopy(1, i).start()

        each(rows)

    def out_copy():
        return pltpu.make_async_copy(act2.at[far, pl.ds(0, width)], out, out_sem.at[0])

    def branch_far():
        pl.semaphore_wait(free_sem, 1)

        def send(i, here):
            ag[0, i] = (acc[here] + dot(att_t[:, rows_of(1 - x, i)].T, wo2[...])).astype(bf16)
            xcopy(0, i).start()

        each(send)

    def branch_near():
        for i in range(n_rb):
            r = rows_of(x, i)
            xcopy(0, i).wait_recv()
            at = att_t[:, r].T
            t_buf[:, 0 : at.shape[1]] = at

            def body(cols):
                total = dot(t_buf[:, 0 : at.shape[1]], wo2[:, cols]) + dot(act2[r, :], w_dn2[:, cols])
                total = total + (b_out[cols] + b_down[cols])[None] + r2[r, cols].astype(f32)
                there = act2.at[rows_of(1 - x, i), cols]
                there[...] = (total + there[...].astype(f32)).astype(bf16)

            over(width, WC, body)
        out_copy().start()

    def finish():
        def last(i, here):
            xcopy(1, i).wait_recv()
            _, normed, inv = norm(rows_of(x, i))
            d_hat = (acc[here] + arrived(1, i)[...].astype(f32)) * ln_gain[...][None]
            first = jnp.mean(d_hat, axis=1, keepdims=True)
            second = jnp.mean(d_hat * normed, axis=1, keepdims=True)
            acc[here] = g2[rows_of(x, i)].astype(f32) + inv * (d_hat - first - normed * second)

        each(last)
        pltpu.make_async_copy(acc, grad_in, out_sem.at[1]).start()

    def small_fill():
        n_up = hidden // width
        ones = jnp.ones((8, 2 * half), bf16)
        up = dot(ones, dup2[...])
        for i in range(n_up):
            sm_send[0, i : i + 1] = up[0:1, i * width : (i + 1) * width]
        sm_send[0, n_up : n_up + 1] = dot(ones, g2[...])[0:1]
        bias = dot_nt(ones, dqkv_t[...])
        sm_send[0, 3:4] = bias[0:1, :width]
        sm_send[0, 4:5, 0 : bias.shape[1] - width] = bias[0:1, width:]

    def small(i):
        device = (sib, yp, zp, zm, xp)[i]
        return pltpu.make_async_remote_copy(
            src_ref=sm_send.at[i], dst_ref=sm_recv.at[i], send_sem=sm_ss.at[i], recv_sem=sm_rs.at[i],
            device_id=device, device_id_type=MESH,
        )


    sums[...] = jnp.zeros_like(sums)
    sm_send[0] = jnp.zeros_like(sums)
    loads[0].wait()
    turn_weights()
    loads[1].wait()
    for i in range(n_rb):
        make_hidden(rows_of(x, i))
    for i in range(2, 5):
        loads[i].wait()
    ff_near()
    for i in range(n_rb):
        ff_far(i)
        if i == n_rb - 2:
            r_copy(n_rb - 1, 1 - x).wait_send()
            for k in range(n_g):
                g_copy(k).start()
    loads[5].wait()
    ff_wave(0)

    def turn_of(v, _):
        t = v // len(TURNS)
        for r, stages in enumerate(TURNS):

            @pl.when(lax.rem(v, len(TURNS)) == r)
            def _():
                for k in stages:
                    stage(k, t)

        at = lambda k: pl.when(v == PLAN[k])

        @at("branch_ff")
        def _():
            branch_ff_far()

        @at("free")
        def _():
            pl.semaphore_signal(free_sem, inc=1, device_id=xp, device_id_type=MESH)

        @at("d_up")
        def _():
            d_up_far()

        done = sum(jnp.where(v > k, 1, 0) for k in FF_AT)
        todo = sum(jnp.where(v >= k, 1, 0) for k in FF_AT)

        @pl.when(todo > done)
        def _():
            ff_wave(todo)

        done_h = sum(jnp.where(v > k, 1, 0) for k in HEAD_AT)
        todo_h = sum(jnp.where(v >= k, 1, 0) for k in HEAD_AT)

        @pl.when(todo_h > done_h)
        def _():
            head(done_h)

        @at("branch_far")
        def _():
            for i in range(NP):
                p_at(n_at - NP + i).wait_send()
            branch_far()

        @at("back_far")
        def _():
            back(1 - x)

        @at("back_near")
        def _():
            back(x)

        @at("small")
        def _():
            small_fill()
            sm_send[0, 5:7] = sums[0:2]
            small(0).start()

        for k in range(1, 6):

            @pl.when(v == SMALL_AT[k - 1])
            def _():
                small(k - 1).wait_recv()
                total = sm_send[k - 1] + sm_recv[k - 1]
                if k < 4:
                    sm_send[k] = total
                    small(k).start()
                elif k == 4:
                    small_out[...] = total
                    sm_send[4] = total
                    small(4).start()
                else:
                    small_out[5:7] = total[5:7]

        @at("branch_near")
        def _():
            branch_near()

        @at("finish")
        def _():
            finish()

        return 0

    lax.fori_loop(0, len(TURNS) * (waves + 5), turn_of, 0)

    def drain(w, _):
        cp("A5", w).wait_send()
        cp("G", w).wait()
        local(w).wait()

        @pl.when(inner)
        def _():
            for k in ("A4", "B4", "B5a", "B5b"):
                cp(k, w).wait_send()

        return 0

    lax.fori_loop(0, waves, drain, 0)
    p_ff(n_ff - 2).wait_send()
    p_ff(n_ff - 1).wait_send()
    for i in range(n_rb):
        xcopy(0, i).wait_send()
        xcopy(1, i).wait_send()
    for i in range(n_rb - 1):
        r_copy(i, x).wait_send()
    for i in range(n_g):
        g_copy(i).wait_send()
    for i in range(5):
        small(i).wait_send()
    out_copy().wait()
    pltpu.make_async_copy(acc, grad_in, out_sem.at[1]).wait()


def mega(g_n, r_n, w_qkv, wo, w_up, w_down, *small):
    half, width = g_n.shape
    rows = 2 * half
    hidden = w_down.shape[0]
    heads = wo.shape[0] // HD
    n_g = width // RW
    waves = 2 * n_g + heads // 2
    n_rb = half // 256
    vm = pl.BlockSpec(memory_space=pltpu.VMEM)
    hbm = pl.BlockSpec(memory_space=pl.ANY)
    dma = pltpu.SemaphoreType.DMA
    v16 = lambda *s: pltpu.VMEM(s, bf16)
    v32 = lambda *s: pltpu.VMEM(s, f32)
    return pl.pallas_call(
        functools.partial(mega_kernel, heads),
        in_specs=[hbm] * 6 + [vm] * len(small),
        out_specs=[hbm, hbm, hbm, vm],
        out_shape=[
            jax.ShapeDtypeStruct((waves, 2 * RW, width), bf16),
            jax.ShapeDtypeStruct((half, width), bf16),
            jax.ShapeDtypeStruct((half, width), f32),
            jax.ShapeDtypeStruct((8, width), f32),
        ],
        scratch_shapes=[
            v16(rows, hidden), v16(rows, hidden), v16(rows, width), v16(rows, width), v16(rows, width),
            v16(heads * 3 * HD, width), v16(heads * HD, width), v16(width, hidden), v16(hidden, width),
            v16(waves, RW, width), v16(2, 2, RW, width), v16(NP, 2, RW, width),
            v16(NS, RQ, width), v16(NS, RQ, width), v16(NS, RQ, width), v16(NS, 2 * RQ, width), v16(NS, RQ, width), v16(NS, RQ, width),
            v32(6 * HD, rows), v16(2 * HD, rows), v16(heads * 3 * HD, rows), v16(heads * HD, rows), v16(RW, rows),
            v16(256, heads * 3 * HD), v32(half, width),
            v32(5, 8, width), v32(5, 8, width), v32(8, width),
            dma((len(KINDS), waves)), dma((len(KINDS), waves)), dma((waves,)), dma((N_LOADS,)), dma((n_rb,)), dma((n_rb,)),
            dma((n_g,)), dma((n_g,)), dma((2, n_rb)), dma((2, n_rb)), dma((5,)), dma((5,)), dma((2,))] + [pltpu.SemaphoreType.REGULAR] * 4,
        compiler_params=pltpu.CompilerParams(collective_id=0, has_side_effects=True, vmem_limit_bytes=63 * 2**20),
        name="attention_and_sums",
    )(g_n, r_n, w_qkv, wo, w_up, w_down, *small)


def widen_kernel(
    n_g, n_at, src, out_in, grad_in, small, down, up, qkv, proj, out, grad, g_gain, g_bias, g_qkv, g_out, g_down, g_up,
    buf, wide, wide_q, wide_p, buf_o, buf_g, in_sem, sem, q_sem, p_sem, through_sem,
):
    waves, _, width = src.shape
    hq = 3 * HD
    arrive = [pltpu.make_async_copy(a, b, through_sem.at[i]) for i, (a, b) in enumerate(((out_in, buf_o), (grad_in, buf_g)))]
    leave = [pltpu.make_async_copy(a, b, through_sem.at[2 + i]) for i, (a, b) in enumerate(((buf_o, out), (buf_g, grad)))]
    loads = [pltpu.make_async_copy(src.at[w], buf.at[w], in_sem.at[w]) for w in range(waves)]
    for k in arrive + loads:
        k.start()
    row = lax.broadcasted_iota(jnp.int32, (RW, RW), 0)
    eye = jnp.where(row == lax.broadcasted_iota(jnp.int32, (RW, RW), 1), 1.0, 0.0).astype(bf16)
    slots, busy, used = wide.shape[0], {}, 0
    for a, b in zip(arrive, leave):
        a.wait()
        b.start()

    def free(slot):
        for k in busy.pop(slot, []):
            k.wait()

    def send(slot, copies):
        for k in copies:
            k.start()
        busy[slot] = copies

    for w in range(waves):
        loads[w].wait()
        if n_g <= w < n_g + n_at:
            j = w - n_g
            s = j % 2
            free(("q", s))
            for k in range(width // RW):
                cols = slice(k * RW, (k + 1) * RW)
                both = jnp.concatenate([buf[w, 0:hq, cols], buf[w, RW : RW + hq, cols]], axis=0)
                wide_q[s, cols] = dot_nt(eye, both)
            for c in range(2):
                wide_p[s, c * HD : (c + 1) * HD] = buf[w, c * RW + hq : (c + 1) * RW].astype(f32)
            send(("q", s), [
                pltpu.make_async_copy(wide_q.at[s], qkv.at[:, pl.ds(j * 2 * hq, 2 * hq)], q_sem.at[s]),
                pltpu.make_async_copy(wide_p.at[s], proj.at[pl.ds(j * 2 * HD, 2 * HD)], p_sem.at[s]),
            ])
            continue
        s = used % slots
        used += 1
        free(s)
        copies = []
        for c in range(2):
            if w < n_g:
                for k in range(width // RW):
                    n = c * (width // RW) + k
                    cols = slice(n * RW, (n + 1) * RW)
                    wide[s, :, cols] = dot_nt(eye, buf[w, c * RW : (c + 1) * RW, k * RW : (k + 1) * RW])
                    copies.append(
                        pltpu.make_async_copy(
                            wide.at[s, :, cols], down.at[cols, pl.ds(w * RW, RW)], sem.at[s, n]
                        )
                    )
            else:
                wide[s, :, c * width : (c + 1) * width] = buf[w, c * RW : (c + 1) * RW].astype(f32)
        if w >= n_g:
            copies = [pltpu.make_async_copy(wide.at[s], up.at[pl.ds((w - n_g - n_at) * RW, RW)], sem.at[s, 0])]
        send(s, copies)
    n_up = g_up.shape[0] // width
    for i in range(n_up):
        g_up[i * width : (i + 1) * width] = small[i]
    g_out[...] = small[n_up]
    g_down[...] = small[n_up]
    g_qkv[0:width] = small[3]
    g_qkv[width:] = small[4, 0 : g_qkv.shape[0] - width]
    g_gain[...] = small[5]
    g_bias[...] = small[6]
    for s in list(busy):
        free(s)
    for k in leave:
        k.wait()


def widen(red, out, grad_in, small, hidden):
    waves, _, width = red.shape
    n_g = width // RW
    n_at = waves - 2 * n_g
    vm = pl.BlockSpec(memory_space=pltpu.VMEM)
    hbm = pl.BlockSpec(memory_space=pl.ANY)
    dma = pltpu.SemaphoreType.DMA
    s32 = lambda *s: jax.ShapeDtypeStruct(s, f32)
    return pl.pallas_call(
        functools.partial(widen_kernel, n_g, n_at),
        in_specs=[hbm] * 3 + [vm],
        out_specs=[hbm] * 6 + [vm] * 6,
        out_shape=[
            s32(hidden, width), s32(width, hidden), s32(width, n_at * 6 * HD), s32(n_at * 2 * HD, width),
            jax.ShapeDtypeStruct(out.shape, out.dtype), s32(*grad_in.shape),
            s32(width), s32(width), s32(n_at * 6 * HD), s32(width), s32(width), s32(hidden),
        ],
        scratch_shapes=[
            pltpu.VMEM((waves, 2 * RW, width), bf16), pltpu.VMEM((4, RW, hidden), f32), pltpu.VMEM((2, width, 6 * HD), f32),
            pltpu.VMEM((2, 2 * HD, width), f32), pltpu.VMEM(out.shape, out.dtype), pltpu.VMEM(grad_in.shape, f32),
            dma((waves,)), dma((4, hidden // RW)), dma((2,)), dma((2,)), dma((4,)),
        ],
        compiler_params=pltpu.CompilerParams(vmem_limit_bytes=56 * 2**20),
        name="widen",
    )(red, out, grad_in, small)


def shards(residual, ln_gain, ln_bias, w_qkv, b_qkv, w_out, b_out, w_up, b_up, w_down, b_down, grad_out):
    rows = 2 * residual.shape[0]
    half_rot = ROT // 2
    inverse = 1.0 / np.float32(10000.0) ** (np.arange(half_rot, dtype=np.float32) * np.float32(2.0 / ROT))
    angles = np.arange(rows, dtype=np.float32)[None, :] * inverse[:, None].astype(np.float32)
    cs = jnp.asarray(np.concatenate([np.cos(angles), np.sin(angles)]).astype(np.float32))
    red, out, grad_in, small = mega(
        grad_out, residual, w_qkv, w_out, w_up, w_down, b_qkv, b_up, cs, ln_gain, ln_bias, b_out, b_down
    )
    grad_w_down, grad_w_up, grad_w_qkv, grad_w_out, out, grad_in, gain, bias, gb_qkv, gb_out, gb_down, gb_up = widen(
        red, out, grad_in, small, w_down.shape[0]
    )
    return out, grad_in, gain, bias, grad_w_qkv, gb_qkv, grad_w_out, gb_out, grad_w_up, gb_up, grad_w_down, gb_down


def contract_rows(left, right):
    return lax.dot_general(
        left, right, (((0,), (0,)), ((), ())), preferred_element_type=jnp.float32
    )


def contract_cols(left, right):
    return lax.dot_general(
        left, right, (((1,), (1,)), ((), ())), preferred_element_type=jnp.float32
    )


def turn_heads(heads, cosine, sine):
    half_rot = ROT // 2
    first = heads[:, :, :half_rot]
    second = heads[:, :, half_rot:ROT]
    rest = heads[:, :, ROT:]
    cos_rows = cosine[:, None, :]
    sin_rows = sine[:, None, :]
    return jnp.concatenate(
        [first * cos_rows - second * sin_rows, second * cos_rows + first * sin_rows, rest], axis=2
    )


def undo_turn(heads, cosine, sine):
    half_rot = ROT // 2
    first = heads[:, :, :half_rot]
    second = heads[:, :, half_rot:ROT]
    rest = heads[:, :, ROT:]
    cos_rows = cosine[:, None, :]
    sin_rows = sine[:, None, :]
    return jnp.concatenate(
        [first * cos_rows + second * sin_rows, second * cos_rows - first * sin_rows, rest], axis=2
    )


def shards_any(
    residual, ln_gain, ln_bias, w_qkv, b_qkv, w_out, b_out, w_up, b_up, w_down, b_down, grad_out
):
    rows_here = residual.shape[0]
    head_cols = w_out.shape[0]
    heads_here = head_cols // HD
    resid_wide = residual.astype(jnp.float32)
    average = jnp.mean(resid_wide, axis=1, keepdims=True)
    centered = resid_wide - average
    variance = jnp.mean(centered * centered, axis=1, keepdims=True)
    inv_std = lax.rsqrt(variance + epsilon)
    normed = centered * inv_std
    h_local = (normed * ln_gain + ln_bias).astype(jnp.bfloat16)
    h_full = lax.all_gather(h_local, "tensor", axis=0, tiled=True)
    group_rows = h_full.shape[0]
    seqlen = min(LEN_MAX, group_rows)
    seq_count = group_rows // seqlen
    qkv = jnp.dot(h_full, w_qkv, preferred_element_type=jnp.float32) + b_qkv
    up_lin = jnp.dot(h_full, w_up, preferred_element_type=jnp.float32) + b_up
    act_wide, gelu_back = jax.vjp(functools.partial(jax.nn.gelu, approximate=False), up_lin)
    act = act_wide.astype(jnp.bfloat16)
    cosine, sine = turn_tables(seqlen)
    causal = jnp.arange(seqlen)[:, None] >= jnp.arange(seqlen)[None, :]
    scale = 1.0 / math.sqrt(HD)

    def attend(block):
        queries = turn_heads(block[:, :, 0, :], cosine, sine).astype(jnp.bfloat16)
        key_rows = turn_heads(block[:, :, 1, :], cosine, sine).astype(jnp.bfloat16)
        value_rows = block[:, :, 2, :].astype(jnp.bfloat16)
        scores = (
            jnp.einsum("qhd,khd->hqk", queries, key_rows, preferred_element_type=jnp.float32)
            * scale
        )
        scores = jnp.where(causal[None], scores, -1e30)
        peak = jnp.max(scores, axis=2, keepdims=True)
        raised = jnp.exp(scores - peak)
        totals = jnp.sum(raised, axis=2, keepdims=True)
        probs = raised / totals
        attended = jnp.einsum(
            "hqk,khd->qhd",
            probs.astype(jnp.bfloat16),
            value_rows,
            preferred_element_type=jnp.float32,
        ).astype(jnp.bfloat16)
        log_total = peak[:, :, 0] + jnp.log(totals[:, :, 0])
        return (queries, key_rows, value_rows, attended, log_total)

    blocks = qkv.reshape(seq_count, seqlen, heads_here, 3, HD)
    queries, key_rows, value_rows, attended, log_total = lax.map(attend, blocks)
    attn_rows = attended.reshape(group_rows, head_cols)
    act_part = lax.slice_in_dim(act, 0, lax.axis_size("tensor") * rows_here, axis=0)
    branch = lax.psum_scatter(
        jnp.dot(attn_rows, w_out, preferred_element_type=jnp.float32)
        + jnp.dot(act_part, w_down, preferred_element_type=jnp.float32),
        "tensor",
        scatter_dimension=0,
        tiled=True,
    )
    out = (resid_wide + branch + b_out + b_down).astype(jnp.bfloat16)
    grad_local = grad_out.astype(jnp.float32)
    grad_full = lax.all_gather(grad_out, "tensor", axis=0, tiled=True)
    grad_w_out = contract_rows(attn_rows, grad_full)
    grad_w_down = contract_rows(act, grad_full)
    d_attended = contract_cols(grad_full, w_out).astype(jnp.bfloat16)
    d_act = contract_cols(grad_full, w_down)
    d_up = gelu_back(d_act)[0].astype(jnp.bfloat16)
    grad_b_up = jnp.sum(d_up, axis=0, dtype=jnp.float32)

    def attend_back(items):
        query_part, key_part, value_part, log_part, d_part = items
        scores = (
            jnp.einsum("qhd,khd->hqk", query_part, key_part, preferred_element_type=jnp.float32)
            * scale
        )
        probs = jnp.where(causal[None], jnp.exp(scores - log_part[:, :, None]), 0.0)
        grad_values = jnp.einsum(
            "hqk,qhd->khd", probs.astype(jnp.bfloat16), d_part, preferred_element_type=jnp.float32
        )
        d_probs = jnp.einsum("qhd,khd->hqk", d_part, value_part, preferred_element_type=jnp.float32)
        d_scores = (probs * (d_probs - jnp.sum(d_probs * probs, axis=2, keepdims=True))).astype(
            jnp.bfloat16
        )
        d_query = (
            jnp.einsum("hqk,khd->qhd", d_scores, key_part, preferred_element_type=jnp.float32)
            * scale
        )
        d_key = (
            jnp.einsum("hqk,qhd->khd", d_scores, query_part, preferred_element_type=jnp.float32)
            * scale
        )
        return jnp.stack(
            [undo_turn(d_query, cosine, sine), undo_turn(d_key, cosine, sine), grad_values], axis=2
        )

    d_blocks = d_attended.reshape(seq_count, seqlen, heads_here, HD)
    d_qkv = lax.map(attend_back, (queries, key_rows, value_rows, log_total, d_blocks))
    d_qkv = d_qkv.reshape(group_rows, 3 * head_cols).astype(jnp.bfloat16)
    grad_b_qkv = jnp.sum(d_qkv, axis=0, dtype=jnp.float32)
    grad_w_qkv = contract_rows(h_full, d_qkv)
    grad_w_up = contract_rows(h_full, d_up)
    d_hidden = lax.psum_scatter(
        contract_cols(d_qkv, w_qkv) + contract_cols(d_up, w_up),
        "tensor",
        scatter_dimension=0,
        tiled=True,
    )
    gain_local = jnp.sum(d_hidden * normed, axis=0)
    bias_local = jnp.sum(d_hidden, axis=0)
    d_hat = d_hidden * ln_gain
    grad_in = grad_local + inv_std * (
        d_hat
        - jnp.mean(d_hat, axis=1, keepdims=True)
        - normed * jnp.mean(d_hat * normed, axis=1, keepdims=True)
    )
    out_bias = jnp.sum(grad_full, axis=0, dtype=jnp.float32)
    grad_w_qkv, grad_b_qkv, grad_w_out, grad_w_up, grad_b_up, grad_w_down, grad_b_out = lax.psum(
        (grad_w_qkv, grad_b_qkv, grad_w_out, grad_w_up, grad_b_up, grad_w_down, out_bias), "dp"
    )
    grad_ln_gain, grad_ln_bias = lax.psum((gain_local, bias_local), ("dp", "tensor"))
    return (
        out,
        grad_in,
        grad_ln_gain,
        grad_ln_bias,
        grad_w_qkv,
        grad_b_qkv,
        grad_w_out,
        grad_b_out,
        grad_w_up,
        grad_b_up,
        grad_w_down,
        grad_b_out,
    )


def solution(mesh):
    small_slice = mesh.shape["dp"] == 16 and mesh.shape["tensor"] == 2
    return jax.shard_map(
        shards if small_slice else shards_any,
        mesh=mesh,
        in_specs=(
            P(("dp", "tensor"), None),
            P(),
            P(),
            P(None, "tensor"),
            P("tensor"),
            P("tensor", None),
            P(),
            P(None, "tensor"),
            P("tensor"),
            P("tensor", None),
            P(),
            P(("dp", "tensor"), None),
        ),
        out_specs=(
            P(("dp", "tensor"), None),
            P(("dp", "tensor"), None),
            P(),
            P(),
            P(None, "tensor"),
            P("tensor"),
            P("tensor", None),
            P(),
            P(None, "tensor"),
            P("tensor"),
            P("tensor", None),
            P(),
        ),
        check_vma=False,
    )
```
